512 devices in a mesh: pb: 32 (over x, y, z_hi), dev: 16 (over z_lo, core).
Axes of the slice: x: 4, y: 4, z: 16 (z_hi: 2, z_lo: 8; z = z_hi * 8 + z_lo), core: 2. Of those that a mesh axis runs over, the one named last changes fastest.
Arguments:
- queries: bfloat16 [8192, 4096], P('pb', 'dev'), may hold values from -6 to 6
- query_back: bfloat16 [8192, 4096], P('pb', 'dev'), may hold values from -0.1875 to 0.1875
- documents: bfloat16 [2048, 4096], P('dev', 'pb'), may hold values from -0.09375 to 0.09375
- doc_hidden: bfloat16 [2048, 4096], P('dev', 'pb'), may hold values from -6 to 6
- wa2: bfloat16 [4096, 512], P('pb'), may hold values from -0.09375 to 0.09375
- ws1: bfloat16 [512, 4096], P(None, 'pb'), may hold values from -0.25 to 0.25
- bias: bfloat16 [4096], P('pb'), may hold values from -3 to 3
- noise: bfloat16 [2, 2048, 512], P(None, 'dev'), may hold values from -0.5 to 0.5
- quant_step: float32 [2], replicated, may hold values from 0.3 to 1.5
- lambdas: float32 [2], replicated, may hold values from 0.5 to 2
Outputs:
- grad_wa2: float32 [4096, 512], P('pb')
- grad_ws1: float32 [512, 4096], P(None, 'pb')
- grad_bias: float32 [4096], P('pb')
The draws below stay inside these ranges and needn't reach their ends.
All inputs are finite; a program needn't handle non-finite values.
Results may differ from the reference program's by a relative error of at most 0.013.
Values may be sent and summed in bfloat16 or wider, within the bound.
A program may use at most 64 MiB of HBM per device.

```python
import math
import jax
import jax.numpy as jnp
from jax import lax

E = 4096
H = 4096
L = 512
QPANEL = 256
DOCS = 2048
QUERIES = 8192
N_PB = 32


def strengthened(array, key, source, target, parts, factor):
    owner, partner = [(jnp.arange(array.shape[position]) // (array.shape[position] // parts)).reshape([-1 if axis == position else 1 for axis in range(array.ndim)]) for position in (source, target)]
    chosen = jax.random.permutation(key, parts)[partner]
    strong = (owner == chosen) | (owner == (partner + parts // 2) % parts)
    return jnp.where(strong, factor * array, array)


def block_scale(rng, shape, pieces, smallest, high):
    gain = 1.0
    for axis_at, shards_of in pieces:
        heights = jax.random.uniform(jax.random.fold_in(jax.random.fold_in(rng, 6), axis_at), (shards_of,), jnp.float32, smallest / len(pieces), high / len(pieces))
        gain = gain * jnp.repeat(jnp.exp(heights), shape[axis_at] // shards_of).reshape((-1,) + (1,) * (len(shape) - 1 - axis_at))
    return gain


def gaussian(rng, shape, deviation, bound, split=(), held_as=jnp.bfloat16):
    array = deviation * jax.random.normal(rng, shape, jnp.float32)
    if split:
        array = array * block_scale(rng, shape, split, -0.22, 0.18)
    return jnp.clip(array, -bound, bound).astype(held_as)


def bell_draw_with(own_key, shape, deviation, limit, cuts, heavy, dtype=jnp.bfloat16):
    entries = deviation * jax.random.normal(own_key, shape, jnp.float32)
    if cuts:
        entries = entries * block_scale(own_key, shape, cuts, -0.22, 0.18)
    return jnp.clip(strengthened(entries, jax.random.fold_in(own_key, 3), *heavy), -limit, limit).astype(dtype)


def setup_inputs(seed: int = 0) -> dict:
    key_list = jax.random.split(jax.random.key(seed), 11)
    return {
        "queries": gaussian(key_list[0], (QUERIES, E), 1.0, 6.0, ((0, 32), (1, 16))),
        "query_back": bell_draw_with(key_list[1], (QUERIES, H), H ** -0.5, 0.1875, ((0, 32), (1, 16)), (0, 1, 32, 2.75)),
        "documents": gaussian(key_list[2], (DOCS, E), E ** -0.5, 0.09375, ((0, 16), (1, 32))),
        "doc_hidden": gaussian(key_list[3], (DOCS, H), 1.0, 6.0, ((0, 16), (1, 32))),
        "wa2": gaussian(key_list[4], (H, L), H ** -0.5, 0.09375, ((0, 32),)),
        "ws1": gaussian(key_list[5], (L, H), L ** -0.5, 0.25, ((1, 32),)),
        "bias": gaussian(key_list[6], (H,), 0.5, 3.0, ((0, 32),)),
        "noise": jnp.clip(jax.random.uniform(key_list[7], (2, DOCS, L), jnp.float32, -0.5, 0.5) * block_scale(key_list[7], (2, DOCS, L), ((1, 16),), -0.4, 0.0), -0.5, 0.5).astype(jnp.bfloat16),
        "quant_step": jnp.clip(jnp.exp(jax.random.uniform(key_list[8], (2,), jnp.float32, math.log(0.3), math.log(1.5))), 0.3, 1.5),
        "lambdas": jnp.clip(jnp.exp(jax.random.uniform(key_list[9], (2,), jnp.float32, math.log(0.5), math.log(2.0))), 0.5, 2.0),
    }


def reference(queries, query_back, documents, doc_hidden, wa2, ws1, bias, noise, quant_step, lambdas):
    target_sim = jnp.dot(queries, documents.T, preferred_element_type=jnp.float32)
    latent = jnp.dot(doc_hidden, wa2, preferred_element_type=jnp.float32)
    noisy = latent[None] + quant_step[:, None, None] * noise.astype(jnp.float32)
    noisy_half = noisy.astype(jnp.bfloat16)
    preact = jnp.einsum('ldk,kh->ldh', noisy_half.astype(jnp.float32), ws1.astype(jnp.float32)) + bias.astype(jnp.float32)
    hidden_act = jax.nn.gelu(preact).astype(jnp.bfloat16)
    factor = 1.0 / math.sqrt(QUERIES)
    panels_back = query_back.reshape(N_PB, QPANEL, H)

    def add_panel(running, pair):
        part = jnp.dot(pair[0].T, pair[1], preferred_element_type=jnp.float32).astype(jnp.bfloat16)
        part = lax.optimization_barrier(part)
        return (running + part.astype(jnp.float32), None)
    grad_ws1 = jnp.zeros((L, H), jnp.float32)
    grad_bias = jnp.zeros((H,), jnp.float32)
    dlatent = jnp.zeros((DOCS, L), jnp.float32)
    for index in range(2):
        approx = jnp.dot(query_back, hidden_act[index].T, preferred_element_type=jnp.float32)
        mismatch = ((approx - target_sim) * factor).astype(jnp.bfloat16)
        panels_err = mismatch.reshape(N_PB, QPANEL, DOCS)
        cotangent, _ = lax.scan(add_panel, jnp.zeros((DOCS, H), jnp.float32), (panels_err, panels_back))
        _, pull = jax.vjp(jax.nn.gelu, preact[index])
        dpre = pull(cotangent)[0]
        dpre_half = dpre.astype(jnp.bfloat16)
        grad_ws1 = grad_ws1 + jnp.dot(noisy_half[index].T, dpre_half, preferred_element_type=jnp.float32)
        grad_bias = grad_bias + lax.optimization_barrier(jnp.sum(dpre, axis=0))
        dlatent = dlatent + jnp.dot(dpre_half, ws1.T, preferred_element_type=jnp.float32)
    rate_grad = lax.optimization_barrier(jnp.sum(lambdas[:, None, None] / math.sqrt(DOCS) * 2.0 * noisy / (quant_step[:, None, None] ** 2 + noisy * noisy), axis=0))
    dlatent_half = (dlatent + rate_grad).astype(jnp.bfloat16)
    grad_wa2 = jnp.dot(doc_hidden.T, dlatent_half, preferred_element_type=jnp.float32)
    return (grad_wa2, grad_ws1, grad_bias)
```

```python
import functools
import math

import jax
import jax.numpy as jnp
from jax import lax
from jax.experimental import pallas as pl
from jax.experimental.pallas import tpu as pltpu
from jax.sharding import PartitionSpec as P

MESH = pl.DeviceIdType.MESH
BF, F32 = jnp.bfloat16, jnp.float32
ORDER = [[(st + k) % 4 for k in range(4)] for st in range(4)]
LAST = (((1,), (1,)), ((), ()))
FIRST = (((0,), (0,)), ((), ()))


def dot(a, b, dims=(((1,), (0,)), ((), ()))):
    return lax.dot_general(a, b, dims, preferred_element_type=F32)


def scratch_table(nzl, rows, part, half, docs, latents):
    width, group, cols = 2 * half, docs // 8, latents // 2
    share = latents // 2 // nzl
    group2 = half // 2 // max(nzl // 2, 1)
    dma = pltpu.SemaphoreType.DMA
    cube = (2, 2, 2, 2)
    return dict(
        qb=pltpu.VMEM((2, 2 * nzl, rows, part), BF),
        dbuf=pltpu.VMEM(cube + (docs, width), BF),
        hbuf=pltpu.VMEM(cube + (2 * docs, width), BF),
        sbuf=pltpu.VMEM(cube + (2 * docs, width), BF),
        rb0=pltpu.VMEM((2, 2, 2, 2 * docs, width), BF),
        rb1=pltpu.VMEM((2, 2, 2 * docs, width), BF),
        rb2=pltpu.VMEM((2, 2 * docs, width), BF),
        rb3=pltpu.VMEM((2 * docs, width), BF),
        wp=pltpu.VMEM((latents, width), BF),
        bp=pltpu.VMEM((8, width), F32),
        lps=pltpu.VMEM((16, group, cols), BF),
        lrx=pltpu.VMEM((16, group, cols), BF),
        lzs=pltpu.VMEM((group, cols), BF),
        lzr=pltpu.VMEM((group, cols), BF),
        lat=pltpu.VMEM((16, group, cols), BF),
        rate=pltpu.VMEM((group, cols), F32),
        nh=pltpu.VMEM((2 * docs, latents), BF),
        slope=pltpu.VMEM((2 * docs, width), F32),
        acc=pltpu.VMEM((2 * docs, rows), F32),
        acct=pltpu.VMEM((docs, rows), F32),
        mm=pltpu.VMEM((2 * docs, rows), BF),
        cot=pltpu.VMEM((2 * docs, width), F32),
        dps=pltpu.VMEM((16, group, cols), BF),
        drx=pltpu.VMEM((16, group, cols), BF),
        dzs=pltpu.VMEM((group, cols), BF),
        dzr=pltpu.VMEM((group, cols), BF),
        dla=pltpu.VMEM((16, group, cols), BF),
        dlf=pltpu.VMEM((docs, latents), BF),
        gwx=pltpu.VMEM((2, latents // 2 + 16, width), BF),
        gwy=pltpu.VMEM((latents // 2 + 16, width), BF),
        gws=pltpu.VMEM((2 * nzl, share + 16, half), BF),
        gwr=pltpu.VMEM((2 * nzl, share + 16, half), BF),
        gwo=pltpu.VMEM((nzl, share, half), BF),
        gwp=pltpu.VMEM((nzl, share, half), BF),
        gax=pltpu.VMEM((2, nzl, group2, cols), BF),
        gay=pltpu.VMEM((nzl, group2, cols), BF),
        gas=pltpu.VMEM((nzl, group2, cols), BF),
        gar=pltpu.VMEM((nzl, group2, cols), BF),
        gao=pltpu.VMEM((nzl, group2, cols), BF),
        gap=pltpu.VMEM((nzl, group2, cols), BF),
        zs=dma((2, 2, nzl)),
        zr=dma((2, nzl)),
        cs=dma((2, nzl)),
        cr=dma((2, nzl)),
        ls=dma((16,)),
        lr=dma((16,)),
        las=dma((16,)),
        lar=dma((16,)),
        ds=dma((16,)),
        dr=dma((16,)),
        das=dma((16,)),
        dar=dma((16,)),
        dgs=dma((4, 4)),
        dgr=dma((4, 4)),
        hgs=dma((4, 4)),
        hgr=dma((4, 4)),
        rss=dma((4, 4)),
        rsr=dma((4, 4)),
        ones=dma((10,)),
        oner=dma((10,)),
        gwss=dma((2 * nzl,)),
        gwsr=dma((2 * nzl,)),
        gwas=dma((nzl,)),
        gwar=dma((nzl,)),
        gass=dma((nzl,)),
        gasr=dma((nzl,)),
        gaas=dma((nzl,)),
        gaar=dma((nzl,)),
    )


def body(
    names, nzl, factor, rate_scale,
    q_ref, b_ref, d_ref, dh_ref, wa2_ref, ws1_ref, bias_ref, noise_ref, qs_ref, lam_ref,
    gwa2_ref, gws1_ref, gbias_ref, *scratch,
):
    r = dict(zip(names, scratch))
    docs, half = d_ref.shape
    width = 2 * half
    latents = ws1_ref.shape[0]
    group, cols = r["lps"].shape[1:]
    khalf = latents // 2
    share = khalf // nzl
    group2 = r["gax"].shape[2]

    p, d = lax.axis_index("pb"), lax.axis_index("dev")
    zh, xy = lax.rem(p, 2), lax.div(p, 2)
    x, y = lax.div(xy, 4), lax.rem(xy, 4)
    zl, c = lax.div(d, 2), lax.rem(d, 2)
    z = zh * nzl + zl
    own = (lax.div(x, 2), lax.rem(lax.div(x + 1, 2), 2), lax.div(y, 2), lax.rem(lax.div(y + 1, 2), 2))

    def at(xy_=None, zh_=None, zl_=None, c_=None):
        xy_, zh_ = xy if xy_ is None else xy_, zh if zh_ is None else zh_
        zl_, c_ = zl if zl_ is None else zl_, c if c_ is None else c_
        return (xy_ * 2 + zh_, zl_ * 2 + c_)

    def flip(v):
        return v + 1 - 2 * lax.rem(v, 2)

    across = (
        at(xy_=(3 - x) * 4 + y),
        at(xy_=flip(x) * 4 + y),
        at(xy_=x * 4 + 3 - y),
        at(xy_=x * 4 + flip(y)),
    )
    core = at(c_=1 - c)
    far = at(zh_=1 - zh)
    mirror = at(zh_=1 - zh, zl_=nzl - 1 - zl)

    def rc(src, dst, ssem, rsem, to):
        return pltpu.make_async_remote_copy(
            src_ref=src, dst_ref=dst, send_sem=ssem, recv_sem=rsem, device_id=to, device_id_type=MESH
        )

    def lanes(start, size):
        return pl.ds(pl.multiple_of(start * size, size), size)

    def loop(n, f, first=1):
        def step(k, carry):
            f(k)
            return carry

        lax.fori_loop(first, n, step, 0)

    part = dot(dh_ref[...], wa2_ref[...]).astype(BF)
    for s in range(16):
        g, h = s // 2 * group, s % 2 * cols
        r["lps"][s] = part[g : g + group, h : h + cols]
    r["lrx"][xy] = r["lps"][xy]
    r["qb"][0, d] = b_ref[...]
    r["qb"][1, d] = q_ref[...]
    r["dbuf"][own + (slice(None), lanes(zh, half))] = d_ref[...]
    r["wp"][:, lanes(zh, half)] = ws1_ref[...]
    r["bp"][:, lanes(zh, half)] = bias_ref[...]

    barrier = pltpu.get_barrier_semaphore()

    def hello(to):
        pl.semaphore_signal(barrier, inc=1, device_id=to, device_id_type=MESH)

    loop(16, lambda k: hello(at(xy_=lax.rem(xy + k, 16))))
    loop(2 * nzl, lambda k: hello(at(zh_=lax.div(lax.rem(z + k, 2 * nzl), nzl), zl_=lax.rem(z + k, nzl))))
    hello(core)
    pl.semaphore_wait(barrier, 15 + 2 * nzl - 1 + 1)

    def scatter(src, dst, ssem, rsem):
        def send(k):
            to = lax.rem(xy + k, 16)
            rc(src.at[to], dst.at[xy], ssem.at[k], rsem.at[xy], at(xy_=to)).start()

        loop(16, send)

    def gather(buf, ssem, rsem):
        def send(k):
            rc(buf.at[xy], buf.at[xy], ssem.at[k], rsem.at[xy], at(xy_=lax.rem(xy + k, 16))).start()

        loop(16, send)

    def arrived(buf, ssem, rsem):
        def wait(k):
            src = lax.rem(xy + 16 - k, 16)
            rc(buf.at[src], buf.at[src], ssem.at[k], rsem.at[src], at(xy_=src)).wait_recv()

        loop(16, wait)

    def sent(buf, ssem, rsem):
        loop(16, lambda k: rc(buf.at[xy], buf.at[xy], ssem.at[k], rsem.at[xy], core).wait_send())

    def total(buf):
        value = buf[0].astype(F32)
        for s in range(1, buf.shape[0]):
            value = value + buf[s].astype(F32)
        return value

    def zcopy(stream, block, side, step):
        ref = r["qb"].at[stream, block * 2 + c]
        to = at(zl_=zl + 1) if side == 0 else at(zl_=zl - 1)
        return rc(ref, ref, r["zs"].at[stream, side, step], r["zr"].at[stream, block], to)

    def ccopy(stream, block):
        ref = r["qb"].at[stream, block * 2 + c]
        return rc(ref, ref, r["cs"].at[stream, block], r["cr"].at[stream, block], core)

    def zstep(step):
        for side in range(2) if step else (None,):
            block = zl if side is None else (zl - step if side == 0 else zl + step)

            def service():
                for stream in range(2):
                    if step:
                        zcopy(stream, block, side, step).wait_recv()
                    if side in (None, 0):
                        pl.when(zl < nzl - 1)(lambda: zcopy(stream, block, 0, step).start())
                    if side in (None, 1):
                        pl.when(zl > 0)(lambda: zcopy(stream, block, 1, step).start())
                    ccopy(stream, block).start()

            if side is None:
                service()
            elif step < nzl:
                pl.when((block >= 0) if side == 0 else (block < nzl))(service)

    def zdone():
        for stream in range(2):
            for step in range(nzl):
                pl.when((zl - step >= 0) & (zl < nzl - 1))(lambda: zcopy(stream, zl - step, 0, step).wait_send())
                pl.when((zl + step < nzl) & (zl > 0))(lambda: zcopy(stream, zl + step, 1, step).wait_send())
            loop(nzl, lambda block: ccopy(stream, block).wait_send(), 0)

    def cube(fixed, flipped=()):
        return tuple(1 - own[i] if i in flipped else own[i] if i in fixed else slice(None) for i in range(4))

    def gather_copy(buf, k, st, ssem, rsem, incoming):
        n = buf.shape[4] // 4
        left = ORDER[st][k:]
        idx = cube(left, left[:1] if incoming else ())
        ref = buf.at[idx + (pl.ds(st * n, n),)]
        return rc(ref, ref, ssem.at[k, st], rsem.at[k, st], across[ORDER[st][k]])

    def gather_start(buf, k, ssem, rsem):
        for st in range(4):
            gather_copy(buf, k, st, ssem, rsem, False).start()

    def gather_wait(buf, k, ssem, rsem):
        for st in range(4):
            gather_copy(buf, k, st, ssem, rsem, True).wait_recv()

    def gather_sent(buf, ssem, rsem):
        for k in range(4):
            for st in range(4):
                gather_copy(buf, k, st, ssem, rsem, False).wait_send()

    def one(i, src, dst, to):
        return rc(src, dst, r["ones"].at[i], r["oner"].at[i], to)

    dg = (r["dgs"], r["dgr"])
    hg = (r["hgs"], r["hgr"])
    mine, other = lanes(zh, half), lanes(1 - zh, half)

    scatter(r["lps"], r["lrx"], r["ls"], r["lr"])
    dpiece = lambda side: r["dbuf"].at[own + (slice(None), side)]
    copy_d = one(0, dpiece(mine), dpiece(mine), far)
    copy_d.start()
    wrow = pl.ds(pl.multiple_of(c * khalf, khalf), khalf)
    copy_w = one(1, r["wp"].at[wrow, mine], r["wp"].at[wrow, mine], mirror)
    copy_w.start()
    copy_b = one(2, r["bp"].at[:, mine], r["bp"].at[:, mine], mirror)
    copy_b.start()
    zstep(0)

    arrived(r["lrx"], r["ls"], r["lr"])
    r["lzs"][...] = total(r["lrx"]).astype(BF)
    copy_l = one(3, r["lzs"], r["lzr"], far)
    copy_l.start()
    one(0, dpiece(other), dpiece(other), far).wait_recv()
    gather_start(r["dbuf"], 0, *dg)
    one(1, r["wp"].at[wrow, other], r["wp"].at[wrow, other], mirror).wait_recv()
    copy_wc = one(4, r["wp"].at[wrow, other], r["wp"].at[wrow, other], core)
    copy_wc.start()
    one(2, r["bp"].at[:, other], r["bp"].at[:, other], mirror).wait_recv()
    copy_l.wait_recv()
    block = r["lzs"][...].astype(F32) + r["lzr"][...].astype(F32)
    r["lat"][xy] = block.astype(BF)
    gather(r["lat"], r["las"], r["lar"])
    brow = pl.ds(pl.multiple_of(lax.div(xy, 2) * group, group), group)
    bcol = lanes(lax.rem(xy, 2), cols)
    rate = jnp.zeros_like(block)
    for l in range(2):
        step = qs_ref[l]
        noisy = block + step * noise_ref[l, brow, bcol].astype(F32)
        rate = rate + lam_ref[l] * (2.0 * rate_scale) * noisy / (step * step + noisy * noisy)
    r["rate"][...] = rate
    if nzl > 1:
        zstep(1)
    gather_wait(r["dbuf"], 0, *dg)
    gather_start(r["dbuf"], 1, *dg)
    arrived(r["lat"], r["las"], r["lar"])
    for s in range(16):
        g, h = s // 2 * group, s % 2 * cols
        value = r["lat"][s].astype(F32)
        for l in range(2):
            r["nh"][l * docs + g : l * docs + g + group, h : h + cols] = (
                value + qs_ref[l] * noise_ref[l, g : g + group, h : h + cols].astype(F32)
            ).astype(BF)
    wrow2 = pl.ds(pl.multiple_of((1 - c) * khalf, khalf), khalf)
    one(4, r["wp"].at[wrow2, other], r["wp"].at[wrow2, other], core).wait_recv()

    pre = dot(r["nh"][...], r["wp"][...]) + r["bp"][0:1, :]
    k0 = math.sqrt(2.0 / math.pi)
    t = jnp.tanh(k0 * (pre + 0.044715 * (pre * pre * pre)))
    r["hbuf"][own] = (pre * (0.5 * (1.0 + t))).astype(BF)
    r["slope"][...] = 0.5 * (1.0 + t) + 0.5 * pre * (1.0 - t * t) * (k0 * (1.0 + (3.0 * 0.044715) * pre * pre))
    gather_start(r["hbuf"], 0, *hg)
    for step in range(2, 3):
        if step < nzl:
            zstep(step)
    gather_wait(r["hbuf"], 0, *hg)
    gather_start(r["hbuf"], 1, *hg)
    gather_wait(r["dbuf"], 1, *dg)
    gather_start(r["dbuf"], 2, *dg)
    if 3 < nzl:
        zstep(3)
    gather_wait(r["hbuf"], 1, *hg)
    gather_start(r["hbuf"], 2, *hg)
    gather_wait(r["dbuf"], 2, *dg)
    gather_start(r["dbuf"], 3, *dg)
    if 4 < nzl:
        zstep(4)
    gather_wait(r["hbuf"], 2, *hg)
    gather_start(r["hbuf"], 3, *hg)
    for step in range(5, nzl):
        zstep(step)
    gather_wait(r["dbuf"], 3, *dg)
    gather_wait(r["hbuf"], 3, *hg)

    def core_arrived(blk):
        for stream in range(2):
            ref = r["qb"].at[stream, blk * 2 + 1 - c]
            rc(ref, ref, r["cs"].at[stream, blk], r["cr"].at[stream, blk], core).wait_recv()

    loop(nzl, core_arrived, 0)

    def slot(j):
        jx, jy = j // 4, j % 4
        return (jx // 2, (jx + 1) // 2 % 2, jy // 2, (jy + 1) // 2 % 2)

    wide = 2 * nzl

    def piece(buf, j):
        span = 16 // wide
        if span == 1:
            return buf[slot(j)]
        return jnp.concatenate([buf[slot(j * span + i)] for i in range(span)], axis=1)

    for j in range(wide):
        a = dot(piece(r["hbuf"], j), r["qb"][0, j], LAST)
        b = dot(piece(r["dbuf"], j), r["qb"][1, j], LAST)
        if j == 0:
            r["acc"][...] = a
            r["acct"][...] = b
        else:
            r["acc"][...] += a
            r["acct"][...] += b
    for l in range(2):
        span = slice(l * docs, (l + 1) * docs)
        r["mm"][span, :] = ((r["acc"][span, :] - r["acct"][...]) * factor).astype(BF)

    for j in range(wide):
        value = dot(r["mm"][...], r["qb"][0, j]).astype(BF)
        span = 16 // wide
        for i in range(span):
            r["sbuf"][slot(j * span + i)] = value[:, i * width : (i + 1) * width]

    srows = 2 * docs // 4
    rbs = [r["rb0"], r["rb1"], r["rb2"], r["rb3"]]

    def sum_copy(k, st):
        order = ORDER[st]
        span = pl.ds(st * srows, srows)
        src = r["sbuf"].at[cube(order[: k + 1], order[k : k + 1]) + (span,)]
        dst = rbs[k].at[(slice(None),) * (3 - k) + (span,)]
        return rc(src, dst, r["rss"].at[k, st], r["rsr"].at[k, st], across[order[k]])

    for st in range(4):
        sum_copy(0, st).start()
    for k in range(4):
        for st in range(4):
            span = pl.ds(st * srows, srows)
            sum_copy(k, st).wait_recv()
            idx = cube(ORDER[st][: k + 1]) + (span,)
            got = rbs[k][(slice(None),) * (3 - k) + (span,)]
            value = r["sbuf"][idx].astype(F32) + got.astype(F32)
            if k < 3:
                r["sbuf"][idx] = value.astype(BF)
                sum_copy(k + 1, st).start()
            else:
                r["cot"][span, :] = value

    dpre = r["cot"][...] * r["slope"][...]
    both = dpre[:docs] + dpre[docs:]
    dl = dot(both.astype(BF), r["wp"][...], LAST).astype(BF)
    for s in range(16):
        g, h = s // 2 * group, s % 2 * cols
        r["dps"][s] = dl[g : g + group, h : h + cols]
    r["drx"][xy] = r["dps"][xy]
    scatter(r["dps"], r["drx"], r["ds"], r["dr"])
    gw = dot(r["nh"][...], dpre.astype(BF), FIRST).astype(BF)
    gb = jnp.broadcast_to(jnp.sum(both, axis=0, keepdims=True), (16, width)).astype(BF)
    for i in range(2):
        r["gwx"][i, :khalf, :] = gw[i * khalf : (i + 1) * khalf]
        r["gwx"][i, khalf:, :] = gb
    copy_gw = one(5, r["gwx"].at[1 - c], r["gwy"], core)
    copy_gw.start()

    arrived(r["drx"], r["ds"], r["dr"])
    r["dzs"][...] = total(r["drx"]).astype(BF)
    copy_dl = one(6, r["dzs"], r["dzr"], far)
    copy_dl.start()

    copy_gw.wait_recv()
    gsum = (r["gwx"][c].astype(F32) + r["gwy"][...].astype(F32)).astype(BF)
    for zz in range(2 * nzl):
        row, col = zz % nzl * share, zz // nzl * half
        r["gws"][zz, :share, :] = gsum[row : row + share, col : col + half]
        r["gws"][zz, share:, :] = gsum[khalf:, col : col + half]
    r["gwr"][z] = r["gws"][z]

    def gw_copy(k):
        to = lax.rem(z + k, 2 * nzl)
        target = at(zh_=lax.div(to, nzl), zl_=lax.rem(to, nzl))
        return rc(r["gws"].at[to], r["gwr"].at[z], r["gwss"].at[k], r["gwsr"].at[z], target)

    def gw_wait(k):
        src = lax.rem(z + 2 * nzl - k, 2 * nzl)
        rc(r["gwr"].at[src], r["gwr"].at[src], r["gwss"].at[k], r["gwsr"].at[src], core).wait_recv()

    copy_dl.wait_recv()
    dblock = r["dzs"][...].astype(F32) + r["dzr"][...].astype(F32) + r["rate"][...]
    r["dla"][xy] = dblock.astype(BF)
    gather(r["dla"], r["das"], r["dar"])
    loop(2 * nzl, lambda k: gw_copy(k).start())

    arrived(r["dla"], r["das"], r["dar"])
    for s in range(16):
        g, h = s // 2 * group, s % 2 * cols
        r["dlf"][g : g + group, h : h + cols] = r["dla"][s]
    ga = dot(dh_ref[...], r["dlf"][...], FIRST).astype(BF)
    for i in range(2):
        for zz in range(nzl):
            g, h = i * (half // 2) + zz // 2 * group2, zz % 2 * cols
            r["gax"][i, zz] = ga[g : g + group2, h : h + cols]
    copy_ga = one(7, r["gax"].at[1 - c], r["gay"], core)
    copy_ga.start()

    def line(k):
        return at(zl_=lax.rem(zl + k, nzl))

    def line_gather(buf, ssem, rsem):
        return lambda k: rc(buf.at[zl], buf.at[zl], ssem.at[k], rsem.at[zl], line(k))

    def line_wait(buf, ssem, rsem):
        def wait(k):
            src = lax.rem(zl + nzl - k, nzl)
            rc(buf.at[src], buf.at[src], ssem.at[k], rsem.at[src], core).wait_recv()

        loop(nzl, wait)

    copy_ga.wait_recv()
    for zz in range(nzl):
        r["gas"][zz] = (r["gax"][c, zz].astype(F32) + r["gay"][zz].astype(F32)).astype(BF)
    r["gar"][zl] = r["gas"][zl]

    def ga_copy(k):
        to = lax.rem(zl + k, nzl)
        return rc(r["gas"].at[to], r["gar"].at[zl], r["gass"].at[k], r["gasr"].at[zl], at(zl_=to))

    loop(nzl, lambda k: ga_copy(k).start())
    loop(2 * nzl, gw_wait)
    gwsum = total(r["gwr"])
    gbias_ref[...] = gwsum[share : share + 8]
    r["gwo"][zl] = gwsum[:share].astype(BF)
    gw_out = line_gather(r["gwo"], r["gwas"], r["gwar"])
    loop(nzl, lambda k: gw_out(k).start())

    line_wait(r["gar"], r["gass"], r["gasr"])
    r["gao"][zl] = total(r["gar"]).astype(BF)
    ga_out = line_gather(r["gao"], r["gaas"], r["gaar"])
    loop(nzl, lambda k: ga_out(k).start())

    line_wait(r["gwo"], r["gwas"], r["gwar"])
    copy_gwo = one(8, r["gwo"], r["gwp"], core)
    copy_gwo.start()
    line_wait(r["gao"], r["gaas"], r["gaar"])
    copy_gao = one(9, r["gao"], r["gap"], core)
    copy_gao.start()

    def put_w(base, buf):
        for zz in range(nzl):
            start = pl.multiple_of(base * khalf + zz * share, share)
            gws1_ref[pl.ds(start, share), :] = buf[zz].astype(F32)

    def put_a(base, buf):
        for zz in range(nzl):
            start = pl.multiple_of(base * (half // 2) + zz // 2 * group2, group2)
            gwa2_ref[pl.ds(start, group2), zz % 2 * cols : zz % 2 * cols + cols] = buf[zz].astype(F32)

    put_w(c, r["gwo"])
    put_a(c, r["gao"])
    copy_gwo.wait_recv()
    put_w(1 - c, r["gwp"])
    copy_gao.wait_recv()
    put_a(1 - c, r["gap"])

    sent(r["lps"], r["ls"], r["lr"])
    sent(r["lat"], r["las"], r["lar"])
    sent(r["dps"], r["ds"], r["dr"])
    sent(r["dla"], r["das"], r["dar"])
    zdone()
    gather_sent(r["dbuf"], *dg)
    gather_sent(r["hbuf"], *hg)
    for k in range(4):
        for st in range(4):
            sum_copy(k, st).wait_send()
    for copy in (copy_d, copy_w, copy_b, copy_l, copy_wc, copy_gw, copy_dl, copy_ga, copy_gwo, copy_gao):
        copy.wait_send()
    loop(2 * nzl, lambda k: gw_copy(k).wait_send())
    loop(nzl, lambda k: ga_copy(k).wait_send())
    loop(nzl, lambda k: gw_out(k).wait_send())
    loop(nzl, lambda k: ga_out(k).wait_send())


def per_device(queries, query_back, documents, doc_hidden, wa2, ws1, bias, noise, quant_step, lambdas):
    rows, part = queries.shape
    docs, half = documents.shape
    latents = ws1.shape[0]
    nzl = lax.axis_size("dev") // 2
    n_pb = lax.axis_size("pb")
    table = scratch_table(nzl, rows, part, half, docs, latents)
    vmem = pl.BlockSpec(memory_space=pltpu.VMEM)
    smem = pl.BlockSpec(memory_space=pltpu.SMEM)
    kernel = functools.partial(
        body, tuple(table), nzl, 1.0 / math.sqrt(rows * n_pb), 1.0 / math.sqrt(docs * 2 * nzl)
    )
    gwa2, gws1, gbias = pl.pallas_call(
        kernel,
        out_shape=(
            jax.ShapeDtypeStruct((half, latents), F32),
            jax.ShapeDtypeStruct((latents, half), F32),
            jax.ShapeDtypeStruct((8, half), F32),
        ),
        in_specs=[vmem] * 8 + [smem] * 2,
        out_specs=[vmem] * 3,
        scratch_shapes=list(table.values()),
        compiler_params=pltpu.CompilerParams(
            collective_id=0, has_side_effects=True, vmem_limit_bytes=40 * 1024 * 1024
        ),
    )(
        queries, query_back, documents, doc_hidden, wa2, ws1,
        jnp.broadcast_to(bias.astype(F32)[None], (8, half)), noise, quant_step, lambdas,
    )
    return gwa2, gws1, gbias[0]


def solution(mesh):
    in_specs = (
        P("pb", "dev"),
        P("pb", "dev"),
        P("dev", "pb"),
        P("dev", "pb"),
        P("pb", None),
        P(None, "pb"),
        P("pb"),
        P(None, "dev", None),
        P(),
        P(),
    )
    out_specs = (P("pb", None), P(None, "pb"), P("pb"))
    return jax.shard_map(
        per_device, mesh=mesh, in_specs=in_specs, out_specs=out_specs, check_vma=False
    )
```

```python
import functools
import math

import jax
import jax.numpy as jnp
from jax import lax
from jax.experimental import pallas as pl
from jax.experimental.pallas import tpu as pltpu
from jax.sharding import PartitionSpec as P

MESH = pl.DeviceIdType.MESH
BF, F32 = jnp.bfloat16, jnp.float32
ORDER = [[0, 2, 1, 3], [2, 0, 3, 1], [1, 3, 0, 2], [3, 1, 2, 0]]
LAST = (((1,), (1,)), ((), ()))
FIRST = (((0,), (0,)), ((), ()))


def dot(a, b, dims=(((1,), (0,)), ((), ()))):
    return lax.dot_general(a, b, dims, preferred_element_type=F32)


def scratch_table(nzl, rows, part, half, docs, latents):
    width, group, cols = 2 * half, docs // 8, latents // 2
    share = latents // 2 // nzl
    group2 = half // 2 // max(nzl // 2, 1)
    dma = pltpu.SemaphoreType.DMA
    cube = (2, 2, 2, 2)
    return dict(
        qb=pltpu.VMEM((2, 2 * nzl, rows, part), BF),
        dbuf=pltpu.VMEM(cube + (docs, width), BF),
        hbuf=pltpu.VMEM(cube + (2 * docs, width), BF),
        sbuf=pltpu.VMEM(cube + (2 * docs, width), BF),
        rb0=pltpu.VMEM((2, 2, 2, 2 * docs, width), BF),
        rb1=pltpu.VMEM((2, 2, 2 * docs, width), BF),
        rb2=pltpu.VMEM((3, 2 * docs, width), BF),
        dh=pltpu.VMEM((docs, width), BF),
        wa2=pltpu.VMEM((half, latents), BF),
        noise=pltpu.VMEM((2, docs, latents), BF),
        relay=pltpu.VMEM((docs // 2, half), BF),
        wp=pltpu.VMEM((latents, width), BF),
        bp=pltpu.VMEM((8, width), F32),
        lps=pltpu.VMEM((16, group, cols), BF),
        lrx=pltpu.VMEM((16, group, cols), BF),
        lzs=pltpu.VMEM((group, cols), BF),
        lzr=pltpu.VMEM((group, cols), BF),
        lat=pltpu.VMEM((16, group, cols), BF),
        rate=pltpu.VMEM((group, cols), F32),
        nh=pltpu.VMEM((2 * docs, latents), BF),
        slope=pltpu.VMEM((2 * docs, width), F32),
        acc=pltpu.VMEM((2 * docs, rows), F32),
        acct=pltpu.VMEM((docs, rows), F32),
        mm=pltpu.VMEM((2 * docs, rows), BF),
        cot=pltpu.VMEM((2 * docs, width), F32),
        dps=pltpu.VMEM((16, group, cols), BF),
        drx=pltpu.VMEM((16, group, cols), BF),
        dla=pltpu.VMEM((16, group, cols), BF),
        dlf=pltpu.VMEM((docs, latents), BF),
        gwx=pltpu.VMEM((2, latents // 2 + 16, width), BF),
        gwy=pltpu.VMEM((latents // 2 + 16, width), BF),
        gws=pltpu.VMEM((2 * nzl, share + 16, half), BF),
        gwr=pltpu.VMEM((2 * nzl, share + 16, half), BF),
        gwo=pltpu.VMEM((nzl, share, half), BF),
        gwp=pltpu.VMEM((nzl, share, half), BF),
        gax=pltpu.VMEM((2, 2 * nzl, group2, cols), BF),
        gay=pltpu.VMEM((2 * nzl, group2, cols), BF),
        gas=pltpu.VMEM((2 * nzl, group2, cols), BF),
        gar=pltpu.VMEM((2 * nzl, group2, cols), BF),
        gao=pltpu.VMEM((nzl, group2, cols), BF),
        gap=pltpu.VMEM((nzl, group2, cols), BF),
        zs=dma((4, 2, nzl)),
        zr=dma((4, nzl)),
        cs=dma((4, nzl)),
        cr=dma((4, nzl)),
        ls=dma((16,)),
        lr=dma((16,)),
        las=dma((16,)),
        lar=dma((16,)),
        ds=dma((16,)),
        dr=dma((16,)),
        das=dma((16,)),
        dar=dma((16,)),
        dgs=dma((5, 4)),
        dgr=dma((5, 4)),
        hgs=dma((5, 4)),
        hgr=dma((5, 4)),
        rss=dma((5, 8)),
        rsr=dma((5, 8)),
        ones=dma((12,)),
        oner=dma((12,)),
        gwss=dma((2 * nzl,)),
        gwsr=dma((2 * nzl,)),
        gwas=dma((nzl,)),
        gwar=dma((nzl,)),
        gass=dma((2 * nzl,)),
        gasr=dma((2 * nzl,)),
        gaas=dma((nzl,)),
        gaar=dma((nzl,)),
        loc=dma((7,)),
        loc2=dma((1,)),
    )


def body(
    names, nzl, factor, rate_scale,
    q_ref, b_ref, d_ref, dh_ref, wa2_ref, ws1_ref, bias_ref, noise_ref, qs_ref, lam_ref,
    gwa2_ref, gws1_ref, gbias_ref, *scratch,
):
    r = dict(zip(names, scratch))
    docs, half = d_ref.shape
    width = 2 * half
    latents = ws1_ref.shape[0]
    group, cols = r["lps"].shape[1:]
    khalf = latents // 2
    share = khalf // nzl
    group2 = r["gax"].shape[2]

    p, d = lax.axis_index("pb"), lax.axis_index("dev")
    zh, xy = lax.rem(p, 2), lax.div(p, 2)
    x, y = lax.div(xy, 4), lax.rem(xy, 4)
    zl, c = lax.div(d, 2), lax.rem(d, 2)
    z = zh * nzl + zl
    own = (lax.div(x, 2), lax.rem(lax.div(x + 1, 2), 2), lax.div(y, 2), lax.rem(lax.div(y + 1, 2), 2))

    def at(xy_=None, zh_=None, zl_=None, c_=None):
        xy_, zh_ = xy if xy_ is None else xy_, zh if zh_ is None else zh_
        zl_, c_ = zl if zl_ is None else zl_, c if c_ is None else c_
        return (xy_ * 2 + zh_, zl_ * 2 + c_)

    def flip(v):
        return v + 1 - 2 * lax.rem(v, 2)

    def across(*dims):
        px = 3 - x if 0 in dims else flip(x) if 1 in dims else x
        py = 3 - y if 2 in dims else flip(y) if 3 in dims else y
        return at(xy_=px * 4 + py)

    def ring(steps):
        to = lax.rem(z + steps + 2 * nzl, 2 * nzl)
        return at(zh_=lax.div(to, nzl), zl_=lax.rem(to, nzl))

    core = at(c_=1 - c)
    far = at(zh_=1 - zh)
    mirror = at(zh_=1 - zh, zl_=nzl - 1 - zl)

    def rc(src, dst, ssem, rsem, to):
        return pltpu.make_async_remote_copy(
            src_ref=src, dst_ref=dst, send_sem=ssem, recv_sem=rsem, device_id=to, device_id_type=MESH
        )

    def lanes(start, size):
        return pl.ds(pl.multiple_of(start * size, size), size)

    def loop(n, f, first=1):
        def step(k, carry):
            f(k)
            return carry

        lax.fori_loop(first, n, step, 0)

    mine, other = lanes(zh, half), lanes(1 - zh, half)

    def fetch(i, src, dst):
        copy = pltpu.make_async_copy(src, dst, r["loc"].at[i])
        copy.start()
        return copy

    barrier = pltpu.get_barrier_semaphore()

    def hello(to):
        pl.semaphore_signal(barrier, inc=1, device_id=to, device_id_type=MESH)

    fetched = (
        fetch(0, dh_ref, r["dh"].at[:, mine]),
        fetch(1, wa2_ref, r["wa2"]),
        fetch(2, b_ref, r["qb"].at[0, d]),
        fetch(3, q_ref, r["qb"].at[1, d]),
        fetch(4, d_ref, r["dbuf"].at[own + (slice(None), mine)]),
        fetch(5, ws1_ref, r["wp"].at[:, mine]),
        fetch(6, noise_ref, r["noise"]),
    )
    noise_ref = r["noise"]
    loop(2 * nzl, lambda k: hello(ring(k)))
    loop(16, lambda k: hello(at(xy_=lax.rem(xy + k, 16))))
    hello(core)
    r["bp"][:, mine] = jnp.broadcast_to(bias_ref[...].astype(F32), (8, half))
    fetched[0].wait()
    fetched[1].wait()
    part = dot(r["dh"][:, mine], r["wa2"][...]).astype(BF)
    for s in range(16):
        g, h = s // 2 * group, s % 2 * cols
        r["lps"][s] = part[g : g + group, h : h + cols]
    r["lrx"][xy] = r["lps"][xy]
    for copy in fetched[2:]:
        copy.wait()
    pl.semaphore_wait(barrier, 15 + 2 * nzl - 1 + 1)

    def scatter(src, dst, ssem, rsem):
        def send(k):
            to = lax.rem(xy + k, 16)
            rc(src.at[to], dst.at[xy], ssem.at[k], rsem.at[xy], at(xy_=to)).start()

        loop(16, send)

    def gather(buf, ssem, rsem):
        def send(k):
            rc(buf.at[xy], buf.at[xy], ssem.at[k], rsem.at[xy], at(xy_=lax.rem(xy + k, 16))).start()

        loop(16, send)

    def arrived(buf, ssem, rsem):
        def wait(k):
            src = lax.rem(xy + 16 - k, 16)
            rc(buf.at[src], buf.at[src], ssem.at[k], rsem.at[src], at(xy_=src)).wait_recv()

        loop(16, wait)

    def sent(buf, ssem, rsem):
        loop(16, lambda k: rc(buf.at[xy], buf.at[xy], ssem.at[k], rsem.at[xy], core).wait_send())

    def total(buf):
        value = buf[0].astype(F32)
        for s in range(1, buf.shape[0]):
            value = value + buf[s].astype(F32)
        return value

    prow = q_ref.shape[0] // 2

    def panel(piece, block, core_):
        return r["qb"].at[piece // 2, block * 2 + core_, pl.ds(piece % 2 * prow, prow)]

    def zcopy(piece, block, side, step):
        ref = panel(piece, block, c)
        to = at(zl_=zl + 1) if side == 0 else at(zl_=zl - 1)
        return rc(ref, ref, r["zs"].at[piece, side, step], r["zr"].at[piece, block], to)

    def ccopy(piece, block):
        ref = panel(piece, block, c)
        return rc(ref, ref, r["cs"].at[piece, block], r["cr"].at[piece, block], core)

    def zservice(piece, step, side):
        block = zl if side is None else (zl - step if side == 0 else zl + step)

        def service():
            if step:
                zcopy(piece, block, side, step).wait_recv()
            if side in (None, 0):
                pl.when(zl < nzl - 1)(lambda: zcopy(piece, block, 0, step).start())
            if side in (None, 1):
                pl.when(zl > 0)(lambda: zcopy(piece, block, 1, step).start())
            ccopy(piece, block).start()

        if side is None:
            service()
        else:
            pl.when((block >= 0) if side == 0 else (block < nzl))(service)

    def zstep(step, which):
        if step < nzl:
            for piece in (2 * which, 2 * which + 1):
                for side in (0, 1) if step else (None,):
                    zservice(piece, step, side)

    def zdone():
        for piece in range(4):
            for step in range(nzl):
                pl.when((zl - step >= 0) & (zl < nzl - 1))(lambda: zcopy(piece, zl - step, 0, step).wait_send())
                pl.when((zl + step < nzl) & (zl > 0))(lambda: zcopy(piece, zl + step, 1, step).wait_send())
            loop(nzl, lambda block: ccopy(piece, block).wait_send(), 0)

    def cube(fixed, flipped=()):
        return tuple(1 - own[i] if i in flipped else own[i] if i in fixed else slice(None) for i in range(4))

    def gather_copy(buf, m, st, sems, incoming):
        n, order = buf.shape[4] // 4, ORDER[st]
        if m < 3:
            left, moved = order, ((order[0],), (order[1],), (order[0], order[1]))[m]
        else:
            left, moved = order[m - 1 :], (order[m - 1],)
        ref = buf.at[cube(left, moved if incoming else ()) + (pl.ds(st * n, n),)]
        return rc(ref, ref, sems[0].at[m, st], sems[1].at[m, st], across(*moved))

    PHASES = ((0, 1, 2), (3,), (4,))

    def gather_start(buf, phase, sems):
        for m in PHASES[phase]:
            for st in range(4):
                gather_copy(buf, m, st, sems, False).start()

    def gather_wait(buf, phase, sems):
        for m in PHASES[phase]:
            for st in range(4):
                gather_copy(buf, m, st, sems, True).wait_recv()

    def gather_sent(buf, sems):
        for m in range(5):
            for st in range(4):
                gather_copy(buf, m, st, sems, False).wait_send()

    def one(i, src, dst, to):
        return rc(src, dst, r["ones"].at[i], r["oner"].at[i], to)

    dg = (r["dgs"], r["dgr"])
    hg = (r["hgs"], r["hgr"])
    wrow = pl.ds(pl.multiple_of(c * khalf, khalf), khalf)
    wrow2 = pl.ds(pl.multiple_of((1 - c) * khalf, khalf), khalf)
    depth = lax.min(zl, nzl - 1 - zl)
    inward = at(zl_=jnp.where(zl < nzl // 2, zl + 1, zl - 1))
    wmine, wother = r["wp"].at[wrow, mine], r["wp"].at[wrow, other]
    copy_w0 = rc(wmine, wmine, r["ones"].at[1], r["oner"].at[1], mirror)
    copy_w1 = rc(wother, wother, r["ones"].at[11], r["oner"].at[1], inward)
    copy_wc = one(4, wother, wother, core)

    def wstep(hop):
        def service():
            copy_w1.wait_recv()
            if hop < nzl // 2 - 1:
                copy_w1.start()
            copy_wc.start()

        if hop < nzl // 2:
            pl.when(depth == hop)(service)

    scatter(r["lps"], r["lrx"], r["ls"], r["lr"])
    zstep(0, 0)
    zstep(0, 1)
    hdocs = docs // 2
    top, bottom = pl.ds(0, hdocs), pl.ds(hdocs, hdocs)

    def dpiece(rows_, side):
        return r["dbuf"].at[own + (rows_, side)]

    copy_d = one(0, dpiece(top, mine), dpiece(top, mine), far)
    copy_d2 = one(6, dpiece(bottom, mine), dpiece(bottom, mine), far)
    copy_d.start()
    copy_d2.start()
    pl.when(depth == 0)(lambda: copy_w0.start())
    copy_b = one(2, r["bp"].at[:, mine], r["bp"].at[:, mine], mirror)
    copy_b.start()

    arrived(r["lrx"], r["ls"], r["lr"])
    r["lzs"][...] = total(r["lrx"]).astype(BF)
    copy_l = one(10, r["lzs"], r["lzr"], far)
    copy_l.start()
    zstep(1, 0)
    wstep(0)
    zstep(1, 1)
    zstep(2, 0)
    wstep(1)
    zstep(2, 1)
    copy_l.wait_recv()
    block = r["lzs"][...].astype(F32) + r["lzr"][...].astype(F32)
    r["lat"][xy] = block.astype(BF)
    gather(r["lat"], r["las"], r["lar"])
    brow = pl.ds(pl.multiple_of(lax.div(xy, 2) * group, group), group)
    bcol = lanes(lax.rem(xy, 2), cols)
    rate = jnp.zeros_like(block)
    for l in range(2):
        step = qs_ref[l]
        noisy = block + step * noise_ref[l, brow, bcol].astype(F32)
        rate = rate + lam_ref[l] * rate_scale * noisy / (step * step + noisy * noisy)
    r["rate"][...] = rate
    wstep(2)
    zstep(3, 0)
    one(0, dpiece(top, other), dpiece(top, other), far).wait_recv()
    one(6, dpiece(bottom, other), dpiece(bottom, other), far).wait_recv()
    gather_start(r["dbuf"], 0, dg)
    zstep(3, 1)
    wstep(3)
    arrived(r["lat"], r["las"], r["lar"])
    for s in range(16):
        g, h = s // 2 * group, s % 2 * cols
        value = r["lat"][s].astype(F32)
        for l in range(2):
            r["nh"][l * docs + g : l * docs + g + group, h : h + cols] = (
                value + qs_ref[l] * noise_ref[l, g : g + group, h : h + cols].astype(F32)
            ).astype(BF)
    gather_wait(r["dbuf"], 0, dg)
    gather_start(r["dbuf"], 1, dg)
    one(2, r["bp"].at[:, other], r["bp"].at[:, other], mirror).wait_recv()
    one(4, r["wp"].at[wrow2, other], r["wp"].at[wrow2, other], core).wait_recv()

    pre = dot(r["nh"][...], r["wp"][...]) + r["bp"][0:1, :]
    k0 = math.sqrt(2.0 / math.pi)
    t = jnp.tanh(k0 * (pre + 0.044715 * (pre * pre * pre)))
    r["hbuf"][own] = (pre * (0.5 * (1.0 + t))).astype(BF)
    gather_start(r["hbuf"], 0, hg)
    r["slope"][...] = 0.5 * (1.0 + t) + 0.5 * pre * (1.0 - t * t) * (k0 * (1.0 + (3.0 * 0.044715) * pre * pre))
    gather_wait(r["dbuf"], 1, dg)
    gather_start(r["dbuf"], 2, dg)
    zstep(4, 0)
    zstep(4, 1)
    gather_wait(r["hbuf"], 0, hg)
    gather_start(r["hbuf"], 1, hg)
    zstep(5, 0)
    gather_wait(r["hbuf"], 1, hg)
    gather_start(r["hbuf"], 2, hg)
    zstep(5, 1)
    zstep(6, 0)
    zstep(6, 1)
    zstep(7, 0)
    zstep(7, 1)
    copy_dh = one(9, r["dh"].at[:, mine], r["dh"].at[:, mine], far)
    copy_dh.start()
    gather_wait(r["dbuf"], 2, dg)
    gather_wait(r["hbuf"], 2, hg)

    def core_arrived(blk):
        for piece in range(4):
            ref = panel(piece, blk, 1 - c)
            rc(ref, ref, r["cs"].at[piece, blk], r["cr"].at[piece, blk], core).wait_recv()

    loop(nzl, core_arrived, 0)

    def slot(j):
        jx, jy = j // 4, j % 4
        return (jx // 2, (jx + 1) // 2 % 2, jy // 2, (jy + 1) // 2 % 2)

    wide = 2 * nzl

    def piece(buf, j):
        span = 16 // wide
        if span == 1:
            return buf[slot(j)]
        return jnp.concatenate([buf[slot(j * span + i)] for i in range(span)], axis=1)

    for j in range(wide):
        a = dot(piece(r["hbuf"], j), r["qb"][0, j], LAST)
        b = dot(piece(r["dbuf"], j), r["qb"][1, j], LAST)
        if j == 0:
            r["acc"][...] = a
            r["acct"][...] = b
        else:
            r["acc"][...] += a
            r["acct"][...] += b
    for l in range(2):
        span = slice(l * docs, (l + 1) * docs)
        r["mm"][span, :] = ((r["acc"][span, :] - r["acct"][...]) * factor).astype(BF)

    srows = docs // 4

    def sum_copy(m, q):
        order = ORDER[q % 4]
        span = pl.ds(q * srows, srows)
        if m < 2:
            src, moved = cube(order[: m + 1], order[m : m + 1]), order[m : m + 1]
            dst = r[("rb0", "rb1")[m]].at[(slice(None),) * (3 - m) + (span,)]
        else:
            moved = ((order[2],), (order[3],), (order[2], order[3]))[m - 2]
            src = cube(order, moved)
            dst = r["rb2"].at[m - 2, span]
        return rc(r["sbuf"].at[src + (span,)], dst, r["rss"].at[m, q], r["rsr"].at[m, q], across(*moved))

    for l in range(2):
        for j in range(wide):
            value = dot(r["mm"][l * docs : (l + 1) * docs, :], r["qb"][0, j]).astype(BF)
            span = 16 // wide
            for i in range(span):
                r["sbuf"][slot(j * span + i) + (pl.ds(l * docs, docs),)] = value[:, i * width : (i + 1) * width]
        for q in range(4 * l, 4 * l + 4):
            sum_copy(0, q).start()
    for m in range(2):
        for q in range(8):
            span = pl.ds(q * srows, srows)
            sum_copy(m, q).wait_recv()
            idx = cube(ORDER[q % 4][: m + 1]) + (span,)
            got = r[("rb0", "rb1")[m]][(slice(None),) * (3 - m) + (span,)]
            r["sbuf"][idx] = r["sbuf"][idx] + got
            for later in (1,) if m == 0 else (2, 3, 4):
                sum_copy(later, q).start()
    for q in range(8):
        span = pl.ds(q * srows, srows)
        for m in (2, 3, 4):
            sum_copy(m, q).wait_recv()
        value = r["sbuf"][own + (span,)].astype(F32)
        for m in range(3):
            value = value + r["rb2"][m, span].astype(F32)
        r["cot"][span, :] = value

    dpre = r["cot"][...] * r["slope"][...]
    both = dpre[:docs] + dpre[docs:]
    dl = dot(both.astype(BF), r["wp"][...], LAST).astype(BF)
    for s in range(16):
        g, h = s // 2 * group, s % 2 * cols
        r["dps"][s] = dl[g : g + group, h : h + cols]
    r["drx"][xy] = r["dps"][xy]
    scatter(r["dps"], r["drx"], r["ds"], r["dr"])
    gw = dot(r["nh"][...], dpre.astype(BF), FIRST).astype(BF)
    gb = jnp.broadcast_to(jnp.sum(both, axis=0, keepdims=True), (16, width)).astype(BF)
    for i in range(2):
        r["gwx"][i, :khalf, :] = gw[i * khalf : (i + 1) * khalf]
        r["gwx"][i, khalf:, :] = gb
    copy_gw = one(5, r["gwx"].at[1 - c], r["gwy"], core)
    copy_gw.start()

    arrived(r["drx"], r["ds"], r["dr"])
    r["dla"][xy] = (total(r["drx"]) + r["rate"][...]).astype(BF)
    gather(r["dla"], r["das"], r["dar"])

    copy_gw.wait_recv()
    gsum = (r["gwx"][c].astype(F32) + r["gwy"][...].astype(F32)).astype(BF)
    for zz in range(2 * nzl):
        row, col = zz % nzl * share, zz // nzl * half
        r["gws"][zz, :share, :] = gsum[row : row + share, col : col + half]
        r["gws"][zz, share:, :] = gsum[khalf:, col : col + half]
    r["gwr"][z] = r["gws"][z]

    def gw_copy(k):
        to = lax.rem(z + k, 2 * nzl)
        return rc(r["gws"].at[to], r["gwr"].at[z], r["gwss"].at[k], r["gwsr"].at[z], ring(k))

    def gw_wait(k):
        src = lax.rem(z + 2 * nzl - k, 2 * nzl)
        rc(r["gwr"].at[src], r["gwr"].at[src], r["gwss"].at[k], r["gwsr"].at[src], core).wait_recv()

    loop(2 * nzl, lambda k: gw_copy(k).start())
    one(9, r["dh"].at[:, other], r["dh"].at[:, other], far).wait_recv()

    arrived(r["dla"], r["das"], r["dar"])
    for s in range(16):
        g, h = s // 2 * group, s % 2 * cols
        r["dlf"][g : g + group, h : h + cols] = r["dla"][s]
    ga = dot(r["dh"][...], r["dlf"][...], FIRST).astype(BF)
    for i in range(2):
        for zz in range(2 * nzl):
            g, h = zz // nzl * half + i * (half // 2) + zz % nzl // 2 * group2, zz % 2 * cols
            r["gax"][i, zz] = ga[g : g + group2, h : h + cols]
    copy_ga = one(7, r["gax"].at[1 - c], r["gay"], core)
    copy_ga.start()

    def line(k):
        return at(zl_=lax.rem(zl + k, nzl))

    def line_gather(buf, ssem, rsem):
        return lambda k: rc(buf.at[zl], buf.at[zl], ssem.at[k], rsem.at[zl], line(k))

    def line_wait(buf, ssem, rsem):
        def wait(k):
            src = lax.rem(zl + nzl - k, nzl)
            rc(buf.at[src], buf.at[src], ssem.at[k], rsem.at[src], core).wait_recv()

        loop(nzl, wait)

    copy_ga.wait_recv()
    for zz in range(2 * nzl):
        r["gas"][zz] = (r["gax"][c, zz].astype(F32) + r["gay"][zz].astype(F32)).astype(BF)
    r["gar"][z] = r["gas"][z]

    def ga_copy(k):
        to = lax.rem(z + k, 2 * nzl)
        return rc(r["gas"].at[to], r["gar"].at[z], r["gass"].at[k], r["gasr"].at[z], ring(k))

    def ga_wait(k):
        src = lax.rem(z + 2 * nzl - k, 2 * nzl)
        rc(r["gar"].at[src], r["gar"].at[src], r["gass"].at[k], r["gasr"].at[src], core).wait_recv()

    loop(2 * nzl, lambda k: ga_copy(k).start())
    loop(2 * nzl, gw_wait)
    gwsum = total(r["gwr"])
    gbias_ref[...] = gwsum[share : share + 1]
    r["gwo"][zl] = gwsum[:share].astype(BF)
    gw_out = line_gather(r["gwo"], r["gwas"], r["gwar"])
    loop(nzl, lambda k: gw_out(k).start())

    loop(2 * nzl, ga_wait)
    r["gao"][zl] = total(r["gar"]).astype(BF)
    ga_out = line_gather(r["gao"], r["gaas"], r["gaar"])
    loop(nzl, lambda k: ga_out(k).start())

    line_wait(r["gwo"], r["gwas"], r["gwar"])
    copy_gwo = one(8, r["gwo"], r["gwp"], core)
    copy_gwo.start()
    line_wait(r["gao"], r["gaas"], r["gaar"])
    copy_gao = rc(r["gao"], r["gap"], r["gaas"].at[0], r["loc2"].at[0], core)
    copy_gao.start()

    def put_w(base, buf):
        for zz in range(nzl):
            start = pl.multiple_of(base * khalf + zz * share, share)
            gws1_ref[pl.ds(start, share), :] = buf[zz].astype(F32)

    def put_a(base, buf):
        for zz in range(nzl):
            start = pl.multiple_of(base * (half // 2) + zz // 2 * group2, group2)
            gwa2_ref[pl.ds(start, group2), zz % 2 * cols : zz % 2 * cols + cols] = buf[zz].astype(F32)

    put_w(c, r["gwo"])
    put_a(c, r["gao"])
    copy_gwo.wait_recv()
    put_w(1 - c, r["gwp"])
    copy_gao.wait_recv()
    put_a(1 - c, r["gap"])

    sent(r["lps"], r["ls"], r["lr"])
    sent(r["lat"], r["las"], r["lar"])
    sent(r["dps"], r["ds"], r["dr"])
    sent(r["dla"], r["das"], r["dar"])
    zdone()
    gather_sent(r["dbuf"], dg)
    gather_sent(r["hbuf"], hg)
    for m in range(5):
        for q in range(8):
            sum_copy(m, q).wait_send()
    pl.when(depth == 0)(lambda: copy_w0.wait_send())
    pl.when(depth < nzl // 2 - 1)(lambda: copy_w1.wait_send())
    for copy in (copy_d, copy_d2, copy_b, copy_l, copy_wc, copy_dh, copy_gw, copy_ga, copy_gwo, copy_gao):
        copy.wait_send()
    loop(2 * nzl, lambda k: gw_copy(k).wait_send())
    loop(2 * nzl, lambda k: ga_copy(k).wait_send())
    loop(nzl, lambda k: gw_out(k).wait_send())
    loop(nzl, lambda k: ga_out(k).wait_send())


def per_device(queries, query_back, documents, doc_hidden, wa2, ws1, bias, noise, quant_step, lambdas):
    rows, part = queries.shape
    docs, half = documents.shape
    latents = ws1.shape[0]
    nzl = lax.axis_size("dev") // 2
    n_pb = lax.axis_size("pb")
    table = scratch_table(nzl, rows, part, half, docs, latents)
    vmem = pl.BlockSpec(memory_space=pltpu.VMEM)
    hbm = pl.BlockSpec(memory_space=pltpu.HBM)
    smem = pl.BlockSpec(memory_space=pltpu.SMEM)
    kernel = functools.partial(
        body, tuple(table), nzl, 1.0 / math.sqrt(rows * n_pb), 1.0 / math.sqrt(docs * 2 * nzl)
    )
    gwa2, gws1, gbias = pl.pallas_call(
        kernel,
        out_shape=(
            jax.ShapeDtypeStruct((half, latents), F32),
            jax.ShapeDtypeStruct((latents, half), F32),
            jax.ShapeDtypeStruct((1, half), F32),
        ),
        in_specs=[hbm] * 6 + [vmem, hbm] + [smem] * 2,
        out_specs=[vmem] * 3,
        scratch_shapes=list(table.values()),
        compiler_params=pltpu.CompilerParams(
            collective_id=0, has_side_effects=True, vmem_limit_bytes=63 * 1024 * 1024
        ),
    )(
        queries, query_back, documents, doc_hidden, wa2, ws1,
        bias.reshape(1, half), noise, quant_step, lambdas,
    )
    return gwa2, gws1, gbias.reshape(half)


def solution(mesh):
    in_specs = (
        P("pb", "dev"),
        P("pb", "dev"),
        P("dev", "pb"),
        P("dev", "pb"),
        P("pb", None),
        P(None, "pb"),
        P("pb"),
        P(None, "dev", None),
        P(),
        P(),
    )
    out_specs = (P("pb", None), P(None, "pb"), P("pb"))
    return jax.shard_map(
        per_device, mesh=mesh, in_specs=in_specs, out_specs=out_specs, check_vma=False
    )
```

```python
import functools
import math

import jax
import jax.numpy as jnp
from jax import lax
from jax.experimental import pallas as pl
from jax.experimental.pallas import tpu as pltpu
from jax.sharding import PartitionSpec as P

MESH = pl.DeviceIdType.MESH
BF, F32 = jnp.bfloat16, jnp.float32
ORDER = [[0, 2, 1, 3], [2, 0, 3, 1], [1, 3, 0, 2], [3, 1, 2, 0]]
LAST = (((1,), (1,)), ((), ()))
FIRST = (((0,), (0,)), ((), ()))


def dot(a, b, dims=(((1,), (0,)), ((), ()))):
    return lax.dot_general(a, b, dims, preferred_element_type=F32)


def scratch_table(nzl, rows, part, half, docs, latents):
    width, group, cols = 2 * half, docs // 8, latents // 2
    share = latents // 2 // nzl
    group2 = half // 2 // max(nzl // 2, 1)
    dma = pltpu.SemaphoreType.DMA
    cube = (2, 2, 2, 2)
    return dict(
        qb=pltpu.VMEM((2, 2 * nzl, rows, part), BF),
        dbuf=pltpu.VMEM(cube + (docs, width), BF),
        hbuf=pltpu.VMEM(cube + (2 * docs, width), BF),
        sbuf=pltpu.VMEM(cube + (2 * docs, width), BF),
        rb0=pltpu.VMEM((2, 2, 2, 2 * docs, width), BF),
        rb1=pltpu.VMEM((2, 2, 2 * docs, width), BF),
        rb2=pltpu.VMEM((3, 2 * docs, width), BF),
        dh=pltpu.VMEM((docs, width), BF),
        wa2=pltpu.VMEM((half, latents), BF),
        noise=pltpu.VMEM((2, docs, latents), BF),
        wp=pltpu.VMEM((latents, width), BF),
        bp=pltpu.VMEM((8, width), F32),
        lps=pltpu.VMEM((16, group, cols), BF),
        lrx=pltpu.VMEM((16, group, cols), BF),
        lzs=pltpu.VMEM((group, cols), BF),
        lzr=pltpu.VMEM((group, cols), BF),
        lat=pltpu.VMEM((16, group, cols), BF),
        rate=pltpu.VMEM((group, cols), F32),
        nh=pltpu.VMEM((2 * docs, latents), BF),
        slope=pltpu.VMEM((2 * docs, width), F32),
        acc=pltpu.VMEM((2 * docs, rows), F32),
        acct=pltpu.VMEM((docs, rows), F32),
        mm=pltpu.VMEM((2 * docs, rows), BF),
        cot=pltpu.VMEM((2 * docs, width), F32),
        dps=pltpu.VMEM((16, group, cols), BF),
        drx=pltpu.VMEM((16, group, cols), BF),
        dla=pltpu.VMEM((16, group, cols), BF),
        dlf=pltpu.VMEM((docs, latents), BF),
        gwx=pltpu.VMEM((2, latents // 2 + 16, width), BF),
        gwy=pltpu.VMEM((latents // 2 + 16, width), BF),
        gws=pltpu.VMEM((2 * nzl, share + 16, half), BF),
        gwr=pltpu.VMEM((2 * nzl, share + 16, half), BF),
        gwo=pltpu.VMEM((nzl, share, half), BF),
        gwp=pltpu.VMEM((nzl, share, half), BF),
        gax=pltpu.VMEM((2, 2 * nzl, group2, cols), BF),
        gay=pltpu.VMEM((2 * nzl, group2, cols), BF),
        gas=pltpu.VMEM((2 * nzl, group2, cols), BF),
        gar=pltpu.VMEM((2 * nzl, group2, cols), BF),
        gao=pltpu.VMEM((nzl, group2, cols), BF),
        gap=pltpu.VMEM((nzl, group2, cols), BF),
        zs=dma((2, 2, nzl)),
        zr=dma((2, nzl)),
        cs=dma((2, nzl)),
        cr=dma((2, nzl)),
        ls=dma((16,)),
        lr=dma((16,)),
        las=dma((16,)),
        lar=dma((16,)),
        ds=dma((16,)),
        dr=dma((16,)),
        das=dma((16,)),
        dar=dma((16,)),
        dgs=dma((5, 4)),
        dgr=dma((5, 4)),
        hgs=dma((5, 4)),
        hgr=dma((5, 4)),
        rss=dma((5, 8)),
        rsr=dma((5, 8)),
        ones=dma((12,)),
        oner=dma((12,)),
        gwss=dma((2 * nzl,)),
        gwsr=dma((2 * nzl,)),
        gwas=dma((nzl,)),
        gwar=dma((nzl,)),
        gass=dma((2 * nzl,)),
        gasr=dma((2 * nzl,)),
        gaas=dma((nzl,)),
        gaar=dma((nzl,)),
        loc=dma((7,)),
        loc2=dma((1,)),
    )


def body(
    names, nzl, factor, rate_scale,
    q_ref, b_ref, d_ref, dh_ref, wa2_ref, ws1_ref, bias_ref, noise_ref, qs_ref, lam_ref,
    gwa2_ref, gws1_ref, gbias_ref, *scratch,
):
    r = dict(zip(names, scratch))
    docs, half = d_ref.shape
    width = 2 * half
    latents = ws1_ref.shape[0]
    group, cols = r["lps"].shape[1:]
    khalf = latents // 2
    share = khalf // nzl
    group2 = r["gax"].shape[2]

    p, d = lax.axis_index("pb"), lax.axis_index("dev")
    zh, xy = lax.rem(p, 2), lax.div(p, 2)
    x, y = lax.div(xy, 4), lax.rem(xy, 4)
    zl, c = lax.div(d, 2), lax.rem(d, 2)
    z = zh * nzl + zl
    own = (lax.div(x, 2), lax.rem(lax.div(x + 1, 2), 2), lax.div(y, 2), lax.rem(lax.div(y + 1, 2), 2))

    def at(xy_=None, zh_=None, zl_=None, c_=None):
        xy_, zh_ = xy if xy_ is None else xy_, zh if zh_ is None else zh_
        zl_, c_ = zl if zl_ is None else zl_, c if c_ is None else c_
        return (xy_ * 2 + zh_, zl_ * 2 + c_)

    def flip(v):
        return v + 1 - 2 * lax.rem(v, 2)

    def across(*dims):
        px = 3 - x if 0 in dims else flip(x) if 1 in dims else x
        py = 3 - y if 2 in dims else flip(y) if 3 in dims else y
        return at(xy_=px * 4 + py)

    def ring(steps):
        to = lax.rem(z + steps + 2 * nzl, 2 * nzl)
        return at(zh_=lax.div(to, nzl), zl_=lax.rem(to, nzl))

    core = at(c_=1 - c)
    far = at(zh_=1 - zh)
    mirror = at(zh_=1 - zh, zl_=nzl - 1 - zl)

    def rc(src, dst, ssem, rsem, to):
        return pltpu.make_async_remote_copy(
            src_ref=src, dst_ref=dst, send_sem=ssem, recv_sem=rsem, device_id=to, device_id_type=MESH
        )

    def lanes(start, size):
        return pl.ds(pl.multiple_of(start * size, size), size)

    def loop(n, f, first=1):
        def step(k, carry):
            f(k)
            return carry

        lax.fori_loop(first, n, step, 0)

    mine, other = lanes(zh, half), lanes(1 - zh, half)

    def fetch(i, src, dst):
        copy = pltpu.make_async_copy(src, dst, r["loc"].at[i])
        copy.start()
        return copy

    barrier = pltpu.get_barrier_semaphore()

    def hello(to):
        pl.semaphore_signal(barrier, inc=1, device_id=to, device_id_type=MESH)

    fetched = (
        fetch(0, dh_ref, r["dh"].at[:, mine]),
        fetch(1, wa2_ref, r["wa2"]),
        fetch(2, b_ref, r["qb"].at[0, d]),
        fetch(3, q_ref, r["qb"].at[1, d]),
        fetch(4, d_ref, r["dbuf"].at[own + (slice(None), mine)]),
        fetch(5, ws1_ref, r["wp"].at[:, mine]),
        fetch(6, noise_ref, r["noise"]),
    )
    noise_ref = r["noise"]
    loop(2 * nzl, lambda k: hello(ring(k)))
    loop(16, lambda k: hello(at(xy_=lax.rem(xy + k, 16))))
    hello(core)
    r["bp"][:, mine] = jnp.broadcast_to(bias_ref[...].astype(F32), (8, half))
    fetched[0].wait()
    fetched[1].wait()
    part = dot(r["dh"][:, mine], r["wa2"][...]).astype(BF)
    for s in range(16):
        g, h = s // 2 * group, s % 2 * cols
        r["lps"][s] = part[g : g + group, h : h + cols]
    r["lrx"][xy] = r["lps"][xy]
    for copy in fetched[2:]:
        copy.wait()
    pl.semaphore_wait(barrier, 15 + 2 * nzl - 1 + 1)

    def scatter(src, dst, ssem, rsem):
        def send(k):
            to = lax.rem(xy + k, 16)
            rc(src.at[to], dst.at[xy], ssem.at[k], rsem.at[xy], at(xy_=to)).start()

        loop(16, send)

    def gather(buf, ssem, rsem):
        def send(k):
            rc(buf.at[xy], buf.at[xy], ssem.at[k], rsem.at[xy], at(xy_=lax.rem(xy + k, 16))).start()

        loop(16, send)

    def arrived(buf, ssem, rsem):
        def wait(k):
            src = lax.rem(xy + 16 - k, 16)
            rc(buf.at[src], buf.at[src], ssem.at[k], rsem.at[src], at(xy_=src)).wait_recv()

        loop(16, wait)

    def sent(buf, ssem, rsem):
        loop(16, lambda k: rc(buf.at[xy], buf.at[xy], ssem.at[k], rsem.at[xy], core).wait_send())

    def total(buf):
        value = buf[0].astype(F32)
        for s in range(1, buf.shape[0]):
            value = value + buf[s].astype(F32)
        return value

    def panel(piece, block, core_):
        return r["qb"].at[piece, block * 2 + core_]

    def zcopy(piece, block, side, step):
        ref = panel(piece, block, c)
        to = at(zl_=zl + 1) if side == 0 else at(zl_=zl - 1)
        return rc(ref, ref, r["zs"].at[piece, side, step], r["zr"].at[piece, block], to)

    def ccopy(piece, block):
        ref = panel(piece, block, c)
        return rc(ref, ref, r["cs"].at[piece, block], r["cr"].at[piece, block], core)

    def zservice(piece, step, side):
        block = zl if side is None else (zl - step if side == 0 else zl + step)

        def service():
            if step:
                zcopy(piece, block, side, step).wait_recv()
            if side in (None, 0):
                pl.when(zl < nzl - 1)(lambda: zcopy(piece, block, 0, step).start())
            if side in (None, 1):
                pl.when(zl > 0)(lambda: zcopy(piece, block, 1, step).start())
            ccopy(piece, block).start()

        if side is None:
            service()
        else:
            pl.when((block >= 0) if side == 0 else (block < nzl))(service)

    def zstep(step, which):
        if step < nzl:
            for side in (0, 1) if step else (None,):
                zservice(which, step, side)

    def zdone():
        for piece in range(2):
            for step in range(nzl):
                pl.when((zl - step >= 0) & (zl < nzl - 1))(lambda: zcopy(piece, zl - step, 0, step).wait_send())
                pl.when((zl + step < nzl) & (zl > 0))(lambda: zcopy(piece, zl + step, 1, step).wait_send())
            loop(nzl, lambda block: ccopy(piece, block).wait_send(), 0)

    def cube(fixed, flipped=()):
        return tuple(1 - own[i] if i in flipped else own[i] if i in fixed else slice(None) for i in range(4))

    def gather_copy(buf, m, st, sems, incoming):
        n, order = buf.shape[4] // 4, ORDER[st]
        if m < 3:
            left, moved = order, ((order[0],), (order[1],), (order[0], order[1]))[m]
        else:
            left, moved = order[m - 1 :], (order[m - 1],)
        ref = buf.at[cube(left, moved if incoming else ()) + (pl.ds(st * n, n),)]
        return rc(ref, ref, sems[0].at[m, st], sems[1].at[m, st], across(*moved))

    PHASES = ((0, 1, 2), (3,), (4,))

    def gather_start(buf, phase, sems):
        for m in PHASES[phase]:
            for st in range(4):
                gather_copy(buf, m, st, sems, False).start()

    def gather_wait(buf, phase, sems):
        for m in PHASES[phase]:
            for st in range(4):
                gather_copy(buf, m, st, sems, True).wait_recv()

    def gather_sent(buf, sems):
        for m in range(5):
            for st in range(4):
                gather_copy(buf, m, st, sems, False).wait_send()

    def one(i, src, dst, to):
        return rc(src, dst, r["ones"].at[i], r["oner"].at[i], to)

    dg = (r["dgs"], r["dgr"])
    hg = (r["hgs"], r["hgr"])
    wrow = pl.ds(pl.multiple_of(c * khalf, khalf), khalf)
    wrow2 = pl.ds(pl.multiple_of((1 - c) * khalf, khalf), khalf)
    depth = lax.min(zl, nzl - 1 - zl)
    inward = at(zl_=jnp.where(zl < nzl // 2, zl + 1, zl - 1))
    wmine, wother = r["wp"].at[wrow, mine], r["wp"].at[wrow, other]
    copy_w0 = rc(wmine, wmine, r["ones"].at[1], r["oner"].at[1], mirror)
    copy_w1 = rc(wother, wother, r["ones"].at[11], r["oner"].at[1], inward)
    copy_wc = one(4, wother, wother, core)

    def wstep(hop):
        def service():
            copy_w1.wait_recv()
            if hop < nzl // 2 - 1:
                copy_w1.start()
            copy_wc.start()

        if hop < nzl // 2:
            pl.when(depth == hop)(service)

    scatter(r["lps"], r["lrx"], r["ls"], r["lr"])
    zstep(0, 0)
    zstep(0, 1)
    hdocs = docs // 2
    top, bottom = pl.ds(0, hdocs), pl.ds(hdocs, hdocs)

    def dpiece(rows_, side):
        return r["dbuf"].at[own + (rows_, side)]

    copy_d = one(0, dpiece(top, mine), dpiece(top, mine), far)
    copy_d2 = one(6, dpiece(bottom, mine), dpiece(bottom, mine), far)
    pl.when(depth == 0)(lambda: copy_w0.start())
    copy_b = one(2, r["bp"].at[:, mine], r["bp"].at[:, mine], mirror)
    copy_b.start()

    arrived(r["lrx"], r["ls"], r["lr"])
    r["lzs"][...] = total(r["lrx"]).astype(BF)
    copy_l = one(10, r["lzs"], r["lzr"], far)
    copy_l.start()
    zstep(1, 0)
    wstep(0)
    zstep(1, 1)
    zstep(2, 0)
    wstep(1)
    zstep(2, 1)
    copy_l.wait_recv()
    block = r["lzs"][...].astype(F32) + r["lzr"][...].astype(F32)
    r["lat"][xy] = block.astype(BF)
    gather(r["lat"], r["las"], r["lar"])
    copy_d.start()
    copy_d2.start()
    brow = pl.ds(pl.multiple_of(lax.div(xy, 2) * group, group), group)
    bcol = lanes(lax.rem(xy, 2), cols)
    rate = jnp.zeros_like(block)
    for l in range(2):
        step = qs_ref[l]
        noisy = block + step * noise_ref[l, brow, bcol].astype(F32)
        rate = rate + lam_ref[l] * rate_scale * noisy / (step * step + noisy * noisy)
    r["rate"][...] = rate
    wstep(2)
    zstep(3, 0)
    zstep(3, 1)
    wstep(3)
    arrived(r["lat"], r["las"], r["lar"])
    for s in range(16):
        g, h = s // 2 * group, s % 2 * cols
        value = r["lat"][s].astype(F32)
        for l in range(2):
            r["nh"][l * docs + g : l * docs + g + group, h : h + cols] = (
                value + qs_ref[l] * noise_ref[l, g : g + group, h : h + cols].astype(F32)
            ).astype(BF)
    one(2, r["bp"].at[:, other], r["bp"].at[:, other], mirror).wait_recv()
    one(4, r["wp"].at[wrow2, other], r["wp"].at[wrow2, other], core).wait_recv()

    pre = dot(r["nh"][...], r["wp"][...]) + r["bp"][0:1, :]
    k0 = math.sqrt(2.0 / math.pi)
    t = jnp.tanh(k0 * (pre + 0.044715 * (pre * pre * pre)))
    r["hbuf"][own] = (pre * (0.5 * (1.0 + t))).astype(BF)
    gather_start(r["hbuf"], 0, hg)
    r["slope"][...] = 0.5 * (1.0 + t) + 0.5 * pre * (1.0 - t * t) * (k0 * (1.0 + (3.0 * 0.044715) * pre * pre))
    one(0, dpiece(top, other), dpiece(top, other), far).wait_recv()
    one(6, dpiece(bottom, other), dpiece(bottom, other), far).wait_recv()
    gather_start(r["dbuf"], 0, dg)
    zstep(4, 0)
    zstep(4, 1)
    gather_wait(r["hbuf"], 0, hg)
    gather_start(r["hbuf"], 1, hg)
    gather_wait(r["dbuf"], 0, dg)
    gather_start(r["dbuf"], 1, dg)
    zstep(5, 0)
    gather_wait(r["hbuf"], 1, hg)
    gather_start(r["hbuf"], 2, hg)
    gather_wait(r["dbuf"], 1, dg)
    gather_start(r["dbuf"], 2, dg)
    zstep(5, 1)
    zstep(6, 0)
    zstep(6, 1)
    zstep(7, 0)
    zstep(7, 1)
    copy_dh = one(9, r["dh"].at[:, mine], r["dh"].at[:, mine], far)
    copy_dh.start()
    gather_wait(r["hbuf"], 2, hg)

    def core_arrived(piece):
        def wait(blk):
            ref = panel(piece, blk, 1 - c)
            rc(ref, ref, r["cs"].at[piece, blk], r["cr"].at[piece, blk], core).wait_recv()

        loop(nzl, wait, 0)

    def slot(j):
        jx, jy = j // 4, j % 4
        return (jx // 2, (jx + 1) // 2 % 2, jy // 2, (jy + 1) // 2 % 2)

    wide = 2 * nzl

    def piece(buf, j):
        span = 16 // wide
        if span == 1:
            return buf[slot(j)]
        return jnp.concatenate([buf[slot(j * span + i)] for i in range(span)], axis=1)

    def product(left, stream, total_ref):
        for j in range(wide):
            value = dot(piece(left, j), r["qb"][stream, j], LAST)
            if j == 0:
                total_ref[...] = value
            else:
                total_ref[...] += value

    core_arrived(0)
    product(r["hbuf"], 0, r["acc"])
    core_arrived(1)
    gather_wait(r["dbuf"], 2, dg)
    product(r["dbuf"], 1, r["acct"])
    for l in range(2):
        span = slice(l * docs, (l + 1) * docs)
        r["mm"][span, :] = ((r["acc"][span, :] - r["acct"][...]) * factor).astype(BF)

    srows = docs // 4

    def sum_copy(m, q):
        order = ORDER[q % 4]
        span = pl.ds(q * srows, srows)
        if m < 2:
            src, moved = cube(order[: m + 1], order[m : m + 1]), order[m : m + 1]
            dst = r[("rb0", "rb1")[m]].at[(slice(None),) * (3 - m) + (span,)]
        else:
            moved = ((order[2],), (order[3],), (order[2], order[3]))[m - 2]
            src = cube(order, moved)
            dst = r["rb2"].at[m - 2, span]
        return rc(r["sbuf"].at[src + (span,)], dst, r["rss"].at[m, q], r["rsr"].at[m, q], across(*moved))

    for l in range(2):
        for j in range(wide):
            value = dot(r["mm"][l * docs : (l + 1) * docs, :], r["qb"][0, j]).astype(BF)
            span = 16 // wide
            for i in range(span):
                r["sbuf"][slot(j * span + i) + (pl.ds(l * docs, docs),)] = value[:, i * width : (i + 1) * width]
        for q in range(4 * l, 4 * l + 4):
            sum_copy(0, q).start()
    for m in range(2):
        for q in range(8):
            span = pl.ds(q * srows, srows)
            sum_copy(m, q).wait_recv()
            idx = cube(ORDER[q % 4][: m + 1]) + (span,)
            got = r[("rb0", "rb1")[m]][(slice(None),) * (3 - m) + (span,)]
            r["sbuf"][idx] = r["sbuf"][idx] + got
            for later in (1,) if m == 0 else (2, 3, 4):
                sum_copy(later, q).start()
    for q in range(8):
        span = pl.ds(q * srows, srows)
        for m in (2, 3, 4):
            sum_copy(m, q).wait_recv()
        value = r["sbuf"][own + (span,)].astype(F32)
        for m in range(3):
            value = value + r["rb2"][m, span].astype(F32)
        r["cot"][span, :] = value

    dpre = r["cot"][...] * r["slope"][...]
    both = dpre[:docs] + dpre[docs:]
    dl = dot(both.astype(BF), r["wp"][...], LAST).astype(BF)
    for s in range(16):
        g, h = s // 2 * group, s % 2 * cols
        r["dps"][s] = dl[g : g + group, h : h + cols]
    r["drx"][xy] = r["dps"][xy]
    scatter(r["dps"], r["drx"], r["ds"], r["dr"])
    gw = dot(r["nh"][...], dpre.astype(BF), FIRST).astype(BF)
    gb = jnp.broadcast_to(jnp.sum(both, axis=0, keepdims=True), (16, width)).astype(BF)
    for i in range(2):
        r["gwx"][i, :khalf, :] = gw[i * khalf : (i + 1) * khalf]
        r["gwx"][i, khalf:, :] = gb
    copy_gw = one(5, r["gwx"].at[1 - c], r["gwy"], core)
    copy_gw.start()

    arrived(r["drx"], r["ds"], r["dr"])
    r["dla"][xy] = (total(r["drx"]) + r["rate"][...]).astype(BF)
    gather(r["dla"], r["das"], r["dar"])

    copy_gw.wait_recv()
    gsum = (r["gwx"][c].astype(F32) + r["gwy"][...].astype(F32)).astype(BF)
    for zz in range(2 * nzl):
        row, col = zz % nzl * share, zz // nzl * half
        r["gws"][zz, :share, :] = gsum[row : row + share, col : col + half]
        r["gws"][zz, share:, :] = gsum[khalf:, col : col + half]
    r["gwr"][z] = r["gws"][z]

    def gw_copy(k):
        to = lax.rem(z + k, 2 * nzl)
        return rc(r["gws"].at[to], r["gwr"].at[z], r["gwss"].at[k], r["gwsr"].at[z], ring(k))

    def gw_wait(k):
        src = lax.rem(z + 2 * nzl - k, 2 * nzl)
        rc(r["gwr"].at[src], r["gwr"].at[src], r["gwss"].at[k], r["gwsr"].at[src], core).wait_recv()

    loop(2 * nzl, lambda k: gw_copy(k).start())
    one(9, r["dh"].at[:, other], r["dh"].at[:, other], far).wait_recv()

    arrived(r["dla"], r["das"], r["dar"])
    for s in range(16):
        g, h = s // 2 * group, s % 2 * cols
        r["dlf"][g : g + group, h : h + cols] = r["dla"][s]
    ga = dot(r["dh"][...], r["dlf"][...], FIRST).astype(BF)
    for i in range(2):
        for zz in range(2 * nzl):
            g, h = zz // nzl * half + i * (half // 2) + zz % nzl // 2 * group2, zz % 2 * cols
            r["gax"][i, zz] = ga[g : g + group2, h : h + cols]
    copy_ga = one(7, r["gax"].at[1 - c], r["gay"], core)
    copy_ga.start()

    def line(k):
        return at(zl_=lax.rem(zl + k, nzl))

    def line_gather(buf, ssem, rsem):
        return lambda k: rc(buf.at[zl], buf.at[zl], ssem.at[k], rsem.at[zl], line(k))

    def line_wait(buf, ssem, rsem):
        def wait(k):
            src = lax.rem(zl + nzl - k, nzl)
            rc(buf.at[src], buf.at[src], ssem.at[k], rsem.at[src], core).wait_recv()

        loop(nzl, wait)

    copy_ga.wait_recv()
    for zz in range(2 * nzl):
        r["gas"][zz] = (r["gax"][c, zz].astype(F32) + r["gay"][zz].astype(F32)).astype(BF)
    r["gar"][z] = r["gas"][z]

    def ga_copy(k):
        to = lax.rem(z + k, 2 * nzl)
        return rc(r["gas"].at[to], r["gar"].at[z], r["gass"].at[k], r["gasr"].at[z], ring(k))

    def ga_wait(k):
        src = lax.rem(z + 2 * nzl - k, 2 * nzl)
        rc(r["gar"].at[src], r["gar"].at[src], r["gass"].at[k], r["gasr"].at[src], core).wait_recv()

    loop(2 * nzl, lambda k: ga_copy(k).start())
    loop(2 * nzl, gw_wait)
    gwsum = total(r["gwr"])
    gbias_ref[...] = gwsum[share : share + 1]
    r["gwo"][zl] = gwsum[:share].astype(BF)
    gw_out = line_gather(r["gwo"], r["gwas"], r["gwar"])
    loop(nzl, lambda k: gw_out(k).start())

    loop(2 * nzl, ga_wait)
    r["gao"][zl] = total(r["gar"]).astype(BF)
    ga_out = line_gather(r["gao"], r["gaas"], r["gaar"])
    loop(nzl, lambda k: ga_out(k).start())

    line_wait(r["gwo"], r["gwas"], r["gwar"])
    copy_gwo = one(8, r["gwo"], r["gwp"], core)
    copy_gwo.start()
    line_wait(r["gao"], r["gaas"], r["gaar"])
    copy_gao = rc(r["gao"], r["gap"], r["gaas"].at[0], r["loc2"].at[0], core)
    copy_gao.start()

    def put_w(base, buf):
        for zz in range(nzl):
            start = pl.multiple_of(base * khalf + zz * share, share)
            gws1_ref[pl.ds(start, share), :] = buf[zz]

    def put_a(base, buf):
        for zz in range(nzl):
            start = pl.multiple_of(base * (half // 2) + zz // 2 * group2, group2)
            gwa2_ref[pl.ds(start, group2), zz % 2 * cols : zz % 2 * cols + cols] = buf[zz]

    put_w(c, r["gwo"])
    put_a(c, r["gao"])
    copy_gwo.wait_recv()
    put_w(1 - c, r["gwp"])
    copy_gao.wait_recv()
    put_a(1 - c, r["gap"])

    sent(r["lps"], r["ls"], r["lr"])
    sent(r["lat"], r["las"], r["lar"])
    sent(r["dps"], r["ds"], r["dr"])
    sent(r["dla"], r["das"], r["dar"])
    zdone()
    gather_sent(r["dbuf"], dg)
    gather_sent(r["hbuf"], hg)
    for m in range(5):
        for q in range(8):
            sum_copy(m, q).wait_send()
    pl.when(depth == 0)(lambda: copy_w0.wait_send())
    pl.when(depth < nzl // 2 - 1)(lambda: copy_w1.wait_send())
    for copy in (copy_d, copy_d2, copy_b, copy_l, copy_wc, copy_dh, copy_gw, copy_ga, copy_gwo, copy_gao):
        copy.wait_send()
    loop(2 * nzl, lambda k: gw_copy(k).wait_send())
    loop(2 * nzl, lambda k: ga_copy(k).wait_send())
    loop(nzl, lambda k: gw_out(k).wait_send())
    loop(nzl, lambda k: ga_out(k).wait_send())


def widen(a_ref, w_ref, b_ref, a_out, w_out, b_out):
    a_out[...] = a_ref[...].astype(F32)
    w_out[...] = w_ref[...].astype(F32)
    b_out[...] = b_ref[0]


def per_device(queries, query_back, documents, doc_hidden, wa2, ws1, bias, noise, quant_step, lambdas):
    rows, part = queries.shape
    docs, half = documents.shape
    latents = ws1.shape[0]
    nzl = lax.axis_size("dev") // 2
    n_pb = lax.axis_size("pb")
    table = scratch_table(nzl, rows, part, half, docs, latents)
    vmem = pl.BlockSpec(memory_space=pltpu.VMEM)
    hbm = pl.BlockSpec(memory_space=pltpu.HBM)
    smem = pl.BlockSpec(memory_space=pltpu.SMEM)
    kernel = functools.partial(
        body, tuple(table), nzl, 1.0 / math.sqrt(rows * n_pb), 1.0 / math.sqrt(docs * 2 * nzl)
    )
    gwa2, gws1, gbias = pl.pallas_call(
        kernel,
        out_shape=(
            jax.ShapeDtypeStruct((half, latents), BF),
            jax.ShapeDtypeStruct((latents, half), BF),
            jax.ShapeDtypeStruct((1, half), F32),
        ),
        in_specs=[hbm] * 6 + [vmem, hbm] + [smem] * 2,
        out_specs=[vmem] * 3,
        scratch_shapes=list(table.values()),
        compiler_params=pltpu.CompilerParams(
            collective_id=0, has_side_effects=True, vmem_limit_bytes=63 * 1024 * 1024
        ),
    )(
        queries, query_back, documents, doc_hidden, wa2, ws1,
        bias.reshape(1, half), noise, quant_step, lambdas,
    )
    return pl.pallas_call(
        widen,
        out_shape=(
            jax.ShapeDtypeStruct((half, latents), F32),
            jax.ShapeDtypeStruct((latents, half), F32),
            jax.ShapeDtypeStruct((half,), F32),
        ),
        in_specs=[vmem] * 3,
        out_specs=[vmem] * 3,
    )(gwa2, gws1, gbias)


def solution(mesh):
    in_specs = (
        P("pb", "dev"),
        P("pb", "dev"),
        P("dev", "pb"),
        P("dev", "pb"),
        P("pb", None),
        P(None, "pb"),
        P("pb"),
        P(None, "dev", None),
        P(),
        P(),
    )
    out_specs = (P("pb", None), P(None, "pb"), P("pb"))
    return jax.shard_map(
        per_device, mesh=mesh, in_specs=in_specs, out_specs=out_specs, check_vma=False
    )
```

```python
import functools
import math

import jax
import jax.numpy as jnp
from jax import lax
from jax.experimental import pallas as pl
from jax.experimental.pallas import tpu as pltpu
from jax.sharding import PartitionSpec as P

MESH = pl.DeviceIdType.MESH
BF, F32 = jnp.bfloat16, jnp.float32
ORDER = [[0, 2, 1, 3], [2, 0, 3, 1], [1, 3, 0, 2], [3, 1, 2, 0]]
LAST = (((1,), (1,)), ((), ()))
FIRST = (((0,), (0,)), ((), ()))


def dot(a, b, dims=(((1,), (0,)), ((), ()))):
    return lax.dot_general(a, b, dims, preferred_element_type=F32)


def scratch_table(nzl, rows, part, half, docs, latents):
    width, group, cols = 2 * half, docs // 8, latents // 2
    share = latents // 2 // nzl
    group2 = half // 2 // max(nzl // 2, 1)
    dma = pltpu.SemaphoreType.DMA
    cube = (2, 2, 2, 2)
    return dict(
        qb=pltpu.VMEM((2, 2 * nzl, rows, part), BF),
        dbuf=pltpu.VMEM(cube + (docs, width), BF),
        hbuf=pltpu.VMEM(cube + (2 * docs, width), BF),
        sbuf=pltpu.VMEM(cube + (2 * docs, width), BF),
        rb0=pltpu.VMEM((2, 2, 2, 2 * docs, width), BF),
        rb1=pltpu.VMEM((2, 2, 2 * docs, width), BF),
        rb2=pltpu.VMEM((3, 2 * docs, width), BF),
        dh=pltpu.VMEM((docs, width), BF),
        wa2=pltpu.VMEM((half, latents), BF),
        noise=pltpu.VMEM((2, docs, latents), BF),
        wp=pltpu.VMEM((latents, width), BF),
        bp=pltpu.VMEM((8, width), F32),
        lps=pltpu.VMEM((16, group, cols), BF),
        lrx=pltpu.VMEM((16, group, cols), BF),
        lzs=pltpu.VMEM((group, cols), BF),
        lzr=pltpu.VMEM((group, cols), BF),
        lat=pltpu.VMEM((16, group, cols), BF),
        rate=pltpu.VMEM((group, cols), F32),
        nh=pltpu.VMEM((2 * docs, latents), BF),
        slope=pltpu.VMEM((2 * docs, width), F32),
        acc=pltpu.VMEM((2 * docs, rows), F32),
        acct=pltpu.VMEM((docs, rows), F32),
        mm=pltpu.VMEM((2 * docs, rows), BF),
        cot=pltpu.VMEM((2 * docs, width), F32),
        dps=pltpu.VMEM((16, group, cols), BF),
        drx=pltpu.VMEM((16, group, cols), BF),
        dla=pltpu.VMEM((16, group, cols), BF),
        dlf=pltpu.VMEM((docs, latents), BF),
        gwx=pltpu.VMEM((2, latents // 2 + 16, width), BF),
        gwy=pltpu.VMEM((latents // 2 + 16, width), BF),
        gws=pltpu.VMEM((2 * nzl, share + 16, half), BF),
        gwr=pltpu.VMEM((2 * nzl, share + 16, half), BF),
        gwo=pltpu.VMEM((nzl, share, half), BF),
        gwp=pltpu.VMEM((nzl, share, half), BF),
        gax=pltpu.VMEM((2, 2 * nzl, group2, cols), BF),
        gay=pltpu.VMEM((2 * nzl, group2, cols), BF),
        gas=pltpu.VMEM((2 * nzl, group2, cols), BF),
        gar=pltpu.VMEM((2 * nzl, group2, cols), BF),
        gao=pltpu.VMEM((nzl, group2, cols), BF),
        gap=pltpu.VMEM((nzl, group2, cols), BF),
        zs=dma((2, 2, nzl)),
        zr=dma((2, nzl)),
        cs=dma((2, nzl)),
        cr=dma((2, nzl)),
        ls=dma((16,)),
        lr=dma((16,)),
        las=dma((16,)),
        lar=dma((16,)),
        ds=dma((16,)),
        dr=dma((16,)),
        das=dma((16,)),
        dar=dma((16,)),
        dgs=dma((5, 4)),
        dgr=dma((5, 4)),
        hgs=dma((5, 4)),
        hgr=dma((5, 4)),
        rss=dma((5, 8)),
        rsr=dma((5, 8)),
        ones=dma((12,)),
        oner=dma((12,)),
        gwss=dma((2 * nzl,)),
        gwsr=dma((2 * nzl,)),
        gwas=dma((nzl,)),
        gwar=dma((nzl,)),
        gass=dma((2 * nzl,)),
        gasr=dma((2 * nzl,)),
        gaas=dma((nzl,)),
        gaar=dma((nzl,)),
        loc=dma((7,)),
        loc2=dma((1,)),
    )


def body(
    names, nzl, factor, rate_scale,
    q_ref, b_ref, d_ref, dh_ref, wa2_ref, ws1_ref, bias_ref, noise_ref, qs_ref, lam_ref,
    gwa2_ref, gws1_ref, gbias_ref, *scratch,
):
    r = dict(zip(names, scratch))
    docs, half = d_ref.shape
    width = 2 * half
    latents = ws1_ref.shape[0]
    group, cols = r["lps"].shape[1:]
    khalf = latents // 2
    share = khalf // nzl
    group2 = r["gax"].shape[2]

    p, d = lax.axis_index("pb"), lax.axis_index("dev")
    zh, xy = lax.rem(p, 2), lax.div(p, 2)
    x, y = lax.div(xy, 4), lax.rem(xy, 4)
    zl, c = lax.div(d, 2), lax.rem(d, 2)
    z = zh * nzl + zl
    own = (lax.div(x, 2), lax.rem(lax.div(x + 1, 2), 2), lax.div(y, 2), lax.rem(lax.div(y + 1, 2), 2))

    def at(xy_=None, zh_=None, zl_=None, c_=None):
        xy_, zh_ = xy if xy_ is None else xy_, zh if zh_ is None else zh_
        zl_, c_ = zl if zl_ is None else zl_, c if c_ is None else c_
        return (xy_ * 2 + zh_, zl_ * 2 + c_)

    def flip(v):
        return v + 1 - 2 * lax.rem(v, 2)

    def across(*dims):
        px = 3 - x if 0 in dims else flip(x) if 1 in dims else x
        py = 3 - y if 2 in dims else flip(y) if 3 in dims else y
        return at(xy_=px * 4 + py)

    def ring(steps):
        to = lax.rem(z + steps + 2 * nzl, 2 * nzl)
        return at(zh_=lax.div(to, nzl), zl_=lax.rem(to, nzl))

    core = at(c_=1 - c)
    far = at(zh_=1 - zh)
    mirror = at(zh_=1 - zh, zl_=nzl - 1 - zl)

    def rc(src, dst, ssem, rsem, to):
        return pltpu.make_async_remote_copy(
            src_ref=src, dst_ref=dst, send_sem=ssem, recv_sem=rsem, device_id=to, device_id_type=MESH
        )

    def lanes(start, size):
        return pl.ds(pl.multiple_of(start * size, size), size)

    def loop(n, f, first=1):
        def step(k, carry):
            f(k)
            return carry

        lax.fori_loop(first, n, step, 0)

    mine, other = lanes(zh, half), lanes(1 - zh, half)

    def fetch(i, src, dst):
        copy = pltpu.make_async_copy(src, dst, r["loc"].at[i])
        copy.start()
        return copy

    barrier = pltpu.get_barrier_semaphore()

    def hello(to):
        pl.semaphore_signal(barrier, inc=1, device_id=to, device_id_type=MESH)

    fetched = (
        fetch(0, dh_ref, r["dh"].at[:, mine]),
        fetch(1, wa2_ref, r["wa2"]),
        fetch(2, b_ref, r["qb"].at[0, d]),
        fetch(3, q_ref, r["qb"].at[1, d]),
        fetch(4, d_ref, r["dbuf"].at[own + (slice(None), mine)]),
        fetch(5, ws1_ref, r["wp"].at[:, mine]),
        fetch(6, noise_ref, r["noise"]),
    )
    noise_ref = r["noise"]
    loop(2 * nzl, lambda k: hello(ring(k)))
    loop(16, lambda k: hello(at(xy_=lax.rem(xy + k, 16))))
    hello(core)
    r["bp"][:, mine] = jnp.broadcast_to(bias_ref[...].astype(F32), (8, half))
    fetched[0].wait()
    fetched[1].wait()
    part = dot(r["dh"][:, mine], r["wa2"][...]).astype(BF)
    for s in range(16):
        g, h = s // 2 * group, s % 2 * cols
        r["lps"][s] = part[g : g + group, h : h + cols]
    r["lrx"][xy] = r["lps"][xy]
    for copy in fetched[2:]:
        copy.wait()
    pl.semaphore_wait(barrier, 15 + 2 * nzl - 1 + 1)

    def scatter(src, dst, ssem, rsem):
        def send(k):
            to = lax.rem(xy + k, 16)
            rc(src.at[to], dst.at[xy], ssem.at[k], rsem.at[xy], at(xy_=to)).start()

        loop(16, send)

    def gather(buf, ssem, rsem):
        def send(k):
            rc(buf.at[xy], buf.at[xy], ssem.at[k], rsem.at[xy], at(xy_=lax.rem(xy + k, 16))).start()

        loop(16, send)

    def arrived(buf, ssem, rsem):
        def wait(k):
            src = lax.rem(xy + 16 - k, 16)
            rc(buf.at[src], buf.at[src], ssem.at[k], rsem.at[src], at(xy_=src)).wait_recv()

        loop(16, wait)

    def sent(buf, ssem, rsem):
        loop(16, lambda k: rc(buf.at[xy], buf.at[xy], ssem.at[k], rsem.at[xy], core).wait_send())

    def total(buf):
        value = buf[0].astype(F32)
        for s in range(1, buf.shape[0]):
            value = value + buf[s].astype(F32)
        return value

    def panel(piece, block, core_):
        return r["qb"].at[piece, block * 2 + core_]

    def zcopy(piece, block, side, step):
        ref = panel(piece, block, c)
        to = at(zl_=zl + 1) if side == 0 else at(zl_=zl - 1)
        return rc(ref, ref, r["zs"].at[piece, side, step], r["zr"].at[piece, block], to)

    def ccopy(piece, block):
        ref = panel(piece, block, c)
        return rc(ref, ref, r["cs"].at[piece, block], r["cr"].at[piece, block], core)

    def zservice(piece, step, side):
        block = zl if side is None else (zl - step if side == 0 else zl + step)

        def service():
            if step:
                zcopy(piece, block, side, step).wait_recv()
            if side in (None, 0):
                pl.when(zl < nzl - 1)(lambda: zcopy(piece, block, 0, step).start())
            if side in (None, 1):
                pl.when(zl > 0)(lambda: zcopy(piece, block, 1, step).start())
            ccopy(piece, block).start()

        if side is None:
            service()
        else:
            pl.when((block >= 0) if side == 0 else (block < nzl))(service)

    def zstep(step, which):
        if step < nzl:
            for side in (0, 1) if step else (None,):
                zservice(which, step, side)

    def zdone():
        for piece in range(2):
            for step in range(nzl):
                pl.when((zl - step >= 0) & (zl < nzl - 1))(lambda: zcopy(piece, zl - step, 0, step).wait_send())
                pl.when((zl + step < nzl) & (zl > 0))(lambda: zcopy(piece, zl + step, 1, step).wait_send())
            loop(nzl, lambda block: ccopy(piece, block).wait_send(), 0)

    def cube(fixed, flipped=()):
        return tuple(1 - own[i] if i in flipped else own[i] if i in fixed else slice(None) for i in range(4))

    def gather_copy(buf, m, st, sems, incoming):
        n, order = buf.shape[4] // 4, ORDER[st]
        if m < 3:
            left, moved = order, ((order[0],), (order[1],), (order[0], order[1]))[m]
        else:
            left, moved = order[m - 1 :], (order[m - 1],)
        ref = buf.at[cube(left, moved if incoming else ()) + (pl.ds(st * n, n),)]
        return rc(ref, ref, sems[0].at[m, st], sems[1].at[m, st], across(*moved))

    PHASES = ((0, 1, 2), (3,), (4,))

    def gather_start(buf, phase, sems):
        for m in PHASES[phase]:
            for st in range(4):
                gather_copy(buf, m, st, sems, False).start()

    def gather_wait(buf, phase, sems):
        for m in PHASES[phase]:
            for st in range(4):
                gather_copy(buf, m, st, sems, True).wait_recv()

    def gather_sent(buf, sems):
        for m in range(5):
            for st in range(4):
                gather_copy(buf, m, st, sems, False).wait_send()

    def one(i, src, dst, to):
        return rc(src, dst, r["ones"].at[i], r["oner"].at[i], to)

    dg = (r["dgs"], r["dgr"])
    hg = (r["hgs"], r["hgr"])
    wrow = pl.ds(pl.multiple_of(c * khalf, khalf), khalf)
    wrow2 = pl.ds(pl.multiple_of((1 - c) * khalf, khalf), khalf)
    depth = lax.min(zl, nzl - 1 - zl)
    inward = at(zl_=jnp.where(zl < nzl // 2, zl + 1, zl - 1))
    wmine, wother = r["wp"].at[wrow, mine], r["wp"].at[wrow, other]
    copy_w0 = rc(wmine, wmine, r["ones"].at[1], r["oner"].at[1], mirror)
    copy_w1 = rc(wother, wother, r["ones"].at[11], r["oner"].at[1], inward)
    copy_wc = one(4, wother, wother, core)

    def wstep(hop):
        def service():
            copy_w1.wait_recv()
            if hop < nzl // 2 - 1:
                copy_w1.start()
            copy_wc.start()

        if hop < nzl // 2:
            pl.when(depth == hop)(service)

    scatter(r["lps"], r["lrx"], r["ls"], r["lr"])
    zstep(0, 0)
    zstep(0, 1)
    def dpiece(rows_, side):
        return r["dbuf"].at[own + (rows_, side)]

    copy_d = one(0, dpiece(slice(None), mine), dpiece(slice(None), mine), far)
    pl.when(depth == 0)(lambda: copy_w0.start())
    copy_b = one(2, r["bp"].at[:, mine], r["bp"].at[:, mine], mirror)
    copy_b.start()

    arrived(r["lrx"], r["ls"], r["lr"])
    r["lzs"][...] = total(r["lrx"]).astype(BF)
    copy_l = one(10, r["lzs"], r["lzr"], far)
    copy_l.start()
    zstep(1, 0)
    wstep(0)
    zstep(1, 1)
    zstep(2, 0)
    wstep(1)
    zstep(2, 1)
    copy_l.wait_recv()
    block = r["lzs"][...].astype(F32) + r["lzr"][...].astype(F32)
    r["lat"][xy] = block.astype(BF)
    gather(r["lat"], r["las"], r["lar"])
    copy_d.start()
    brow = pl.ds(pl.multiple_of(lax.div(xy, 2) * group, group), group)
    bcol = lanes(lax.rem(xy, 2), cols)
    rate = jnp.zeros_like(block)
    for l in range(2):
        step = qs_ref[l]
        noisy = block + step * noise_ref[l, brow, bcol].astype(F32)
        rate = rate + lam_ref[l] * rate_scale * noisy / (step * step + noisy * noisy)
    r["rate"][...] = rate
    wstep(2)
    zstep(3, 0)
    zstep(3, 1)
    wstep(3)
    arrived(r["lat"], r["las"], r["lar"])
    for s in range(16):
        g, h = s // 2 * group, s % 2 * cols
        value = r["lat"][s].astype(F32)
        for l in range(2):
            r["nh"][l * docs + g : l * docs + g + group, h : h + cols] = (
                value + qs_ref[l] * noise_ref[l, g : g + group, h : h + cols].astype(F32)
            ).astype(BF)
    one(2, r["bp"].at[:, other], r["bp"].at[:, other], mirror).wait_recv()
    one(4, r["wp"].at[wrow2, other], r["wp"].at[wrow2, other], core).wait_recv()

    pre = dot(r["nh"][...], r["wp"][...]) + r["bp"][0:1, :]
    k0 = math.sqrt(2.0 / math.pi)
    t = jnp.tanh(k0 * (pre + 0.044715 * (pre * pre * pre)))
    r["hbuf"][own] = (pre * (0.5 * (1.0 + t))).astype(BF)
    gather_start(r["hbuf"], 0, hg)
    r["slope"][...] = 0.5 * (1.0 + t) + 0.5 * pre * (1.0 - t * t) * (k0 * (1.0 + (3.0 * 0.044715) * pre * pre))
    one(0, dpiece(slice(None), other), dpiece(slice(None), other), far).wait_recv()
    gather_start(r["dbuf"], 0, dg)
    zstep(4, 0)
    zstep(4, 1)
    gather_wait(r["hbuf"], 0, hg)
    gather_start(r["hbuf"], 1, hg)
    gather_wait(r["dbuf"], 0, dg)
    gather_start(r["dbuf"], 1, dg)
    zstep(5, 0)
    gather_wait(r["hbuf"], 1, hg)
    gather_start(r["hbuf"], 2, hg)
    gather_wait(r["dbuf"], 1, dg)
    gather_start(r["dbuf"], 2, dg)
    zstep(5, 1)
    zstep(6, 0)
    zstep(6, 1)
    zstep(7, 0)
    zstep(7, 1)
    copy_dh = one(9, r["dh"].at[:, mine], r["dh"].at[:, mine], far)
    copy_dh.start()
    gather_wait(r["hbuf"], 2, hg)

    def core_arrived(piece):
        def wait(blk):
            ref = panel(piece, blk, 1 - c)
            rc(ref, ref, r["cs"].at[piece, blk], r["cr"].at[piece, blk], core).wait_recv()

        loop(nzl, wait, 0)

    def slot(j):
        jx, jy = j // 4, j % 4
        return (jx // 2, (jx + 1) // 2 % 2, jy // 2, (jy + 1) // 2 % 2)

    wide = 2 * nzl

    def piece(buf, j):
        span = 16 // wide
        if span == 1:
            return buf[slot(j)]
        return jnp.concatenate([buf[slot(j * span + i)] for i in range(span)], axis=1)

    def product(left, stream, total_ref):
        for j in range(wide):
            value = dot(piece(left, j), r["qb"][stream, j], LAST)
            if j == 0:
                total_ref[...] = value
            else:
                total_ref[...] += value

    core_arrived(0)
    product(r["hbuf"], 0, r["acc"])
    core_arrived(1)
    gather_wait(r["dbuf"], 2, dg)
    product(r["dbuf"], 1, r["acct"])
    for l in range(2):
        span = slice(l * docs, (l + 1) * docs)
        r["mm"][span, :] = ((r["acc"][span, :] - r["acct"][...]) * factor).astype(BF)

    srows = docs // 4

    def sum_copy(m, q):
        order = ORDER[q % 4]
        span = pl.ds(q * srows, srows)
        if m < 2:
            src, moved = cube(order[: m + 1], order[m : m + 1]), order[m : m + 1]
            dst = r[("rb0", "rb1")[m]].at[(slice(None),) * (3 - m) + (span,)]
        else:
            moved = ((order[2],), (order[3],), (order[2], order[3]))[m - 2]
            src = cube(order, moved)
            dst = r["rb2"].at[m - 2, span]
        return rc(r["sbuf"].at[src + (span,)], dst, r["rss"].at[m, q], r["rsr"].at[m, q], across(*moved))

    for l in range(2):
        for j in range(wide):
            value = dot(r["mm"][l * docs : (l + 1) * docs, :], r["qb"][0, j]).astype(BF)
            span = 16 // wide
            for i in range(span):
                r["sbuf"][slot(j * span + i) + (pl.ds(l * docs, docs),)] = value[:, i * width : (i + 1) * width]
        for q in range(4 * l, 4 * l + 4):
            sum_copy(0, q).start()
    sent(r["lps"], r["ls"], r["lr"])
    sent(r["lat"], r["las"], r["lar"])
    zdone()
    gather_sent(r["dbuf"], dg)
    gather_sent(r["hbuf"], hg)
    pl.when(depth == 0)(lambda: copy_w0.wait_send())
    pl.when(depth < nzl // 2 - 1)(lambda: copy_w1.wait_send())
    for copy in (copy_d, copy_b, copy_l, copy_wc, copy_dh):
        copy.wait_send()
    for m in range(2):
        for q in range(8):
            span = pl.ds(q * srows, srows)
            sum_copy(m, q).wait_recv()
            idx = cube(ORDER[q % 4][: m + 1]) + (span,)
            got = r[("rb0", "rb1")[m]][(slice(None),) * (3 - m) + (span,)]
            r["sbuf"][idx] = r["sbuf"][idx] + got
            for later in (1,) if m == 0 else (2, 3, 4):
                sum_copy(later, q).start()
    for q in range(8):
        span = pl.ds(q * srows, srows)
        for m in (2, 3, 4):
            sum_copy(m, q).wait_recv()
        value = r["sbuf"][own + (span,)].astype(F32)
        for m in range(3):
            value = value + r["rb2"][m, span].astype(F32)
        r["cot"][span, :] = value

    dpre = r["cot"][...] * r["slope"][...]
    both = dpre[:docs] + dpre[docs:]
    dl = dot(both.astype(BF), r["wp"][...], LAST).astype(BF)
    for s in range(16):
        g, h = s // 2 * group, s % 2 * cols
        r["dps"][s] = dl[g : g + group, h : h + cols]
    r["drx"][xy] = r["dps"][xy]
    scatter(r["dps"], r["drx"], r["ds"], r["dr"])
    gw = dot(r["nh"][...], dpre.astype(BF), FIRST).astype(BF)
    gb = jnp.broadcast_to(jnp.sum(both, axis=0, keepdims=True), (16, width)).astype(BF)
    for i in range(2):
        r["gwx"][i, :khalf, :] = gw[i * khalf : (i + 1) * khalf]
        r["gwx"][i, khalf:, :] = gb
    copy_gw = one(5, r["gwx"].at[1 - c], r["gwy"], core)
    copy_gw.start()

    arrived(r["drx"], r["ds"], r["dr"])
    r["dla"][xy] = (total(r["drx"]) + r["rate"][...]).astype(BF)
    gather(r["dla"], r["das"], r["dar"])

    copy_gw.wait_recv()
    gsum = (r["gwx"][c].astype(F32) + r["gwy"][...].astype(F32)).astype(BF)
    for zz in range(2 * nzl):
        row, col = zz % nzl * share, zz // nzl * half
        r["gws"][zz, :share, :] = gsum[row : row + share, col : col + half]
        r["gws"][zz, share:, :] = gsum[khalf:, col : col + half]
    r["gwr"][z] = r["gws"][z]

    def gw_copy(k):
        to = lax.rem(z + k, 2 * nzl)
        return rc(r["gws"].at[to], r["gwr"].at[z], r["gwss"].at[k], r["gwsr"].at[z], ring(k))

    def gw_wait(k):
        src = lax.rem(z + 2 * nzl - k, 2 * nzl)
        rc(r["gwr"].at[src], r["gwr"].at[src], r["gwss"].at[k], r["gwsr"].at[src], core).wait_recv()

    loop(2 * nzl, lambda k: gw_copy(k).start())
    one(9, r["dh"].at[:, other], r["dh"].at[:, other], far).wait_recv()

    arrived(r["dla"], r["das"], r["dar"])
    for s in range(16):
        g, h = s // 2 * group, s % 2 * cols
        r["dlf"][g : g + group, h : h + cols] = r["dla"][s]
    ga = dot(r["dh"][...], r["dlf"][...], FIRST).astype(BF)
    for i in range(2):
        for zz in range(2 * nzl):
            g, h = zz // nzl * half + i * (half // 2) + zz % nzl // 2 * group2, zz % 2 * cols
            r["gax"][i, zz] = ga[g : g + group2, h : h + cols]
    copy_ga = one(7, r["gax"].at[1 - c], r["gay"], core)
    copy_ga.start()

    def line(k):
        return at(zl_=lax.rem(zl + k, nzl))

    def line_gather(buf, ssem, rsem):
        return lambda k: rc(buf.at[zl], buf.at[zl], ssem.at[k], rsem.at[zl], line(k))

    def line_wait(buf, ssem, rsem):
        def wait(k):
            src = lax.rem(zl + nzl - k, nzl)
            rc(buf.at[src], buf.at[src], ssem.at[k], rsem.at[src], core).wait_recv()

        loop(nzl, wait)

    copy_ga.wait_recv()
    for zz in range(2 * nzl):
        r["gas"][zz] = (r["gax"][c, zz].astype(F32) + r["gay"][zz].astype(F32)).astype(BF)
    r["gar"][z] = r["gas"][z]

    def ga_copy(k):
        to = lax.rem(z + k, 2 * nzl)
        return rc(r["gas"].at[to], r["gar"].at[z], r["gass"].at[k], r["gasr"].at[z], ring(k))

    def ga_wait(k):
        src = lax.rem(z + 2 * nzl - k, 2 * nzl)
        rc(r["gar"].at[src], r["gar"].at[src], r["gass"].at[k], r["gasr"].at[src], core).wait_recv()

    loop(2 * nzl, lambda k: ga_copy(k).start())
    for m in range(5):
        for q in range(8):
            sum_copy(m, q).wait_send()
    sent(r["dps"], r["ds"], r["dr"])
    copy_gw.wait_send()
    loop(2 * nzl, lambda k: gw_copy(k).wait_send())
    loop(2 * nzl, gw_wait)
    gwsum = total(r["gwr"])
    gbias_ref[...] = gwsum[share : share + 1]
    r["gwo"][zl] = gwsum[:share].astype(BF)
    gw_out = line_gather(r["gwo"], r["gwas"], r["gwar"])
    loop(nzl, lambda k: gw_out(k).start())

    loop(2 * nzl, ga_wait)
    r["gao"][zl] = total(r["gar"]).astype(BF)
    ga_out = line_gather(r["gao"], r["gaas"], r["gaar"])
    loop(nzl, lambda k: ga_out(k).start())

    line_wait(r["gwo"], r["gwas"], r["gwar"])
    copy_gwo = one(8, r["gwo"], r["gwp"], core)
    copy_gwo.start()
    line_wait(r["gao"], r["gaas"], r["gaar"])
    copy_gao = rc(r["gao"], r["gap"], r["gaas"].at[0], r["loc2"].at[0], core)
    copy_gao.start()

    def put_w(base, buf):
        for zz in range(nzl):
            start = pl.multiple_of(base * khalf + zz * share, share)
            gws1_ref[pl.ds(start, share), :] = buf[zz]

    def put_a(base, buf):
        for zz in range(nzl):
            start = pl.multiple_of(base * (half // 2) + zz // 2 * group2, group2)
            gwa2_ref[pl.ds(start, group2), zz % 2 * cols : zz % 2 * cols + cols] = buf[zz]

    put_w(c, r["gwo"])
    put_a(c, r["gao"])
    copy_gwo.wait_recv()
    put_w(1 - c, r["gwp"])
    copy_gao.wait_recv()
    put_a(1 - c, r["gap"])

    sent(r["dla"], r["das"], r["dar"])
    for copy in (copy_ga, copy_gwo, copy_gao):
        copy.wait_send()
    loop(2 * nzl, lambda k: ga_copy(k).wait_send())
    loop(nzl, lambda k: gw_out(k).wait_send())
    loop(nzl, lambda k: ga_out(k).wait_send())


def widen(a_ref, w_ref, b_ref, a_out, w_out, b_out):
    a_out[...] = a_ref[...].astype(F32)
    w_out[...] = w_ref[...].astype(F32)
    b_out[...] = b_ref[0]


def per_device(queries, query_back, documents, doc_hidden, wa2, ws1, bias, noise, quant_step, lambdas):
    rows, part = queries.shape
    docs, half = documents.shape
    latents = ws1.shape[0]
    nzl = lax.axis_size("dev") // 2
    n_pb = lax.axis_size("pb")
    table = scratch_table(nzl, rows, part, half, docs, latents)
    vmem = pl.BlockSpec(memory_space=pltpu.VMEM)
    hbm = pl.BlockSpec(memory_space=pltpu.HBM)
    smem = pl.BlockSpec(memory_space=pltpu.SMEM)
    kernel = functools.partial(
        body, tuple(table), nzl, 1.0 / math.sqrt(rows * n_pb), 1.0 / math.sqrt(docs * 2 * nzl)
    )
    gwa2, gws1, gbias = pl.pallas_call(
        kernel,
        out_shape=(
            jax.ShapeDtypeStruct((half, latents), BF),
            jax.ShapeDtypeStruct((latents, half), BF),
            jax.ShapeDtypeStruct((1, half), F32),
        ),
        in_specs=[hbm] * 6 + [vmem, hbm] + [smem] * 2,
        out_specs=[vmem] * 3,
        scratch_shapes=list(table.values()),
        compiler_params=pltpu.CompilerParams(
            collective_id=0, has_side_effects=True, vmem_limit_bytes=63 * 1024 * 1024
        ),
    )(
        queries, query_back, documents, doc_hidden, wa2, ws1,
        bias.reshape(1, half), noise, quant_step, lambdas,
    )
    return pl.pallas_call(
        widen,
        out_shape=(
            jax.ShapeDtypeStruct((half, latents), F32),
            jax.ShapeDtypeStruct((latents, half), F32),
            jax.ShapeDtypeStruct((half,), F32),
        ),
        in_specs=[vmem] * 3,
        out_specs=[vmem] * 3,
    )(gwa2, gws1, gbias)


def solution(mesh):
    in_specs = (
        P("pb", "dev"),
        P("pb", "dev"),
        P("dev", "pb"),
        P("dev", "pb"),
        P("pb", None),
        P(None, "pb"),
        P("pb"),
        P(None, "dev", None),
        P(),
        P(),
    )
    out_specs = (P("pb", None), P(None, "pb"), P("pb"))
    return jax.shard_map(
        per_device, mesh=mesh, in_specs=in_specs, out_specs=out_specs, check_vma=False
    )
```
